512 devices in a mesh: seq: 64 (over x, y, core), head: 8 (over z).
Axes of the slice: x: 4, y: 8, z: 8, core: 2. Of those that a mesh axis runs over, the one named last changes fastest.
Arguments:
- x_stream: bfloat16 [16384, 8192], P(('seq', 'head')), may hold values from -0.59765625 to 0.59765625
- z_stream: bfloat16 [16384, 8192], P(('seq', 'head')), may hold values from -6 to 6
- b_stream: bfloat16 [16384, 1024], P(('seq', 'head')), may hold values from -1.5 to 1.5
- c_stream: bfloat16 [16384, 1024], P(('seq', 'head')), may hold values from -6 to 6
- dt_stream: bfloat16 [16384, 128], P(('seq', 'head')), may hold values from 0 to 1, as said below
- decay_stream: bfloat16 [16384, 128], P(('seq', 'head')), may hold values from -1 to 0, as said below
- kernel_x: bfloat16 [4, 8192], P(None, 'head'), may hold values from -3 to 3
- kernel_b: bfloat16 [4, 1024], P(None, 'head'), may hold values from -3 to 3
- kernel_c: bfloat16 [4, 1024], P(None, 'head'), may hold values from -3 to 3
- skip_gain: float32 [128], P('head'), may hold values from 0.25 to 1.75
- norm_gain: bfloat16 [8192], replicated, may hold values from 0.5 to 1.5
Outputs:
- layer_out: bfloat16 [16384, 8192], P(('seq', 'head'))
The draws below stay inside these ranges and needn't reach their ends.
Inputs may be any that keep to these rules, and one draw needn't show every extreme that they name: `dt_stream`: positive step sizes. `decay_stream`: non-positive log-decays.
All inputs are finite; a program needn't handle non-finite values.
Results may differ from the reference program's by a relative error of at most 0.012.
Values may be sent and summed in bfloat16 or wider, within the bound.
No kernel may reach another device: no remote copies, remote signals or barrier semaphores. Data moves between devices by JAX's collectives and lax.ppermute only.
A program may use at most 128 MiB of HBM per device.

```python
import jax
import jax.numpy as jnp
from jax import lax

MIXER_HEADS = 128
HEAD_DIM = 64
STATE = 128
GROUPS = 8
KERNEL = 4
SPAN = 128
TOK_DEV = 256
SEQUENCE_TOKENS = 16384


def head_rates(key, quick_share, middle_share):
    inner = jax.random.fold_in(key, 101)
    chooser_key, quick_key, middle_key, steady_key = jax.random.split(inner, 4)
    chooser = jax.random.uniform(chooser_key, (MIXER_HEADS,))
    quick_rate = jnp.exp(jax.random.uniform(quick_key, (MIXER_HEADS,), minval=jnp.log(1.0 / 50.0), maxval=jnp.log(1.0 / 30.0)))
    middle_rate = jnp.exp(jax.random.uniform(middle_key, (MIXER_HEADS,), minval=jnp.log(1.0), maxval=jnp.log(3.0))) / TOK_DEV
    steady_rate = jnp.exp(jax.random.uniform(steady_key, (MIXER_HEADS,), minval=jnp.log(0.2), maxval=jnp.log(0.8))) / SEQUENCE_TOKENS
    return jnp.where(chooser < quick_share, quick_rate, jnp.where(chooser < quick_share + middle_share, middle_rate, steady_rate))


def draw_decay_stream(key, part):
    rates = head_rates(key, 0.2, 0.25)
    key = jax.random.fold_in(key, 1)
    first_key, second_key, third_key, fourth_key = jax.random.split(key, 4)
    blocks = SEQUENCE_TOKENS // TOK_DEV
    block_factor = jnp.exp(jax.random.uniform(first_key, (blocks, 1, MIXER_HEADS), minval=jnp.log(0.5), maxval=jnp.log(2.0)))
    token_factor = jnp.exp(jax.random.uniform(second_key, (blocks, TOK_DEV, MIXER_HEADS), minval=jnp.log(0.6), maxval=jnp.log(1.6)))
    stable_level = -(rates * block_factor * token_factor).reshape(SEQUENCE_TOKENS, MIXER_HEADS)
    sudden_spike = jax.random.uniform(third_key, (SEQUENCE_TOKENS, MIXER_HEADS)) < 2.0 / SEQUENCE_TOKENS
    stack_depth = -jax.random.uniform(fourth_key, (SEQUENCE_TOKENS, MIXER_HEADS), minval=0.22, maxval=0.69)
    return jnp.where(sudden_spike, stack_depth, stable_level).astype(jnp.bfloat16)


def draw_dt_stream(key, part):
    rates = head_rates(key, 0.2, 0.25)
    key = jax.random.fold_in(key, 2)
    token_key, block_key = jax.random.split(key, 2)
    blocks = SEQUENCE_TOKENS // TOK_DEV
    factor = jnp.exp(jax.random.uniform(token_key, (SEQUENCE_TOKENS, MIXER_HEADS), minval=jnp.log(0.5), maxval=jnp.log(2.0)))
    amplitude = jnp.exp(jax.random.uniform(block_key, (blocks, 1, MIXER_HEADS), minval=jnp.log(0.05), maxval=jnp.log(1.0)))
    amplitude = jnp.broadcast_to(amplitude, (blocks, TOK_DEV, MIXER_HEADS)).reshape(SEQUENCE_TOKENS, MIXER_HEADS)
    return (jnp.sqrt(2.0 * rates) * factor * amplitude).astype(jnp.bfloat16)


def shard_levels(key, dims, cuts, least, largest):
    level, own = 1.0, jax.random.fold_in(key, 6)
    for position, blocks in cuts:
        steps = jnp.exp(jax.random.uniform(jax.random.fold_in(own, position), (blocks,), jnp.float32, least / len(cuts), largest / len(cuts)))
        level = level * jnp.repeat(steps, dims[position] // blocks).reshape([-1 if axis == position else 1 for axis in range(len(dims))])
    return level


def bell_draw(own_key, shape, deviation, limit, cuts=(), held_as=jnp.bfloat16):
    result = deviation * jax.random.normal(own_key, shape, jnp.float32)
    if cuts:
        result = result * shard_levels(own_key, shape, cuts, -0.22, 0.18)
    return jnp.clip(result, -limit, limit).astype(held_as)


def setup_inputs(seed: int = 0) -> dict:
    arg_keys = jax.random.split(jax.random.key(seed), 12)
    x_stream = bell_draw(arg_keys[0], (SEQUENCE_TOKENS, MIXER_HEADS * HEAD_DIM), 0.1, 0.59765625, ((0, 512),))
    z_stream = bell_draw(arg_keys[1], (SEQUENCE_TOKENS, MIXER_HEADS * HEAD_DIM), 1.0, 6.0, ((0, 512),))
    b_stream = bell_draw(arg_keys[2], (SEQUENCE_TOKENS, GROUPS * STATE), 0.25, 1.5, ((0, 512),))
    c_stream = bell_draw(arg_keys[3], (SEQUENCE_TOKENS, GROUPS * STATE), 1.0, 6.0, ((0, 512),))
    dt_stream = draw_dt_stream(jax.random.fold_in(arg_keys[11], 71), 0)
    decay_stream = draw_decay_stream(jax.random.fold_in(arg_keys[11], 71), 0)
    kernel_x = bell_draw(arg_keys[6], (KERNEL, MIXER_HEADS * HEAD_DIM), KERNEL ** -0.5, 3.0, ((1, 8),))
    kernel_b = bell_draw(arg_keys[7], (KERNEL, GROUPS * STATE), KERNEL ** -0.5, 3.0, ((1, 8),))
    kernel_c = bell_draw(arg_keys[8], (KERNEL, GROUPS * STATE), KERNEL ** -0.5, 3.0, ((1, 8),))
    skip_gain = jnp.clip(1.0 + 0.15 * jax.random.normal(arg_keys[9], (MIXER_HEADS,), jnp.float32), 0.25, 1.75)
    norm_gain = jnp.clip(1.0 + 0.1 * jax.random.normal(arg_keys[10], (MIXER_HEADS * HEAD_DIM,), jnp.float32), 0.5, 1.5).astype(jnp.bfloat16)
    return {"x_stream": x_stream, "z_stream": z_stream, "b_stream": b_stream, "c_stream": c_stream, "dt_stream": dt_stream, "decay_stream": decay_stream, "kernel_x": kernel_x, "kernel_b": kernel_b, "kernel_c": kernel_c, "skip_gain": skip_gain, "norm_gain": norm_gain}


def conv_silu(values, kernel):
    row_count = values.shape[0]
    border = kernel.shape[0] - 1
    padded = jnp.concatenate([jnp.zeros((border, values.shape[1]), values.dtype), values], 0).astype(jnp.float32)
    taps = kernel.astype(jnp.float32)
    total = padded[0:row_count] * taps[0]
    for offset in range(1, kernel.shape[0]):
        total = total + padded[offset:offset + row_count] * taps[offset]
    return jax.nn.silu(total).astype(jnp.bfloat16)

def gated_norm(values, gate_in, gain, group_width):
    gated = values.astype(jnp.float32) * jax.nn.silu(gate_in.astype(jnp.float32))
    row_count, width = gated.shape
    grouped = gated.reshape(row_count, width // group_width, group_width)
    scale = lax.rsqrt(lax.optimization_barrier(jnp.mean(grouped * grouped, axis=-1, keepdims=True)) + 1e-05)
    return ((grouped * scale).reshape(row_count, width) * gain.astype(jnp.float32)).astype(jnp.bfloat16)

def reference(x_stream, z_stream, b_stream, c_stream, dt_stream, decay_stream, kernel_x, kernel_b, kernel_c, skip_gain, norm_gain):
    x_conv = conv_silu(x_stream, kernel_x)
    b_conv = conv_silu(b_stream, kernel_b)
    c_conv = conv_silu(c_stream, kernel_c)
    per_group = MIXER_HEADS // GROUPS
    spans = SEQUENCE_TOKENS // SPAN
    x_blocks = x_conv.reshape(spans, SPAN, GROUPS, per_group, HEAD_DIM)
    b_blocks = b_conv.reshape(spans, SPAN, GROUPS, STATE)
    c_blocks = c_conv.reshape(spans, SPAN, GROUPS, STATE)
    dt_blocks = dt_stream.astype(jnp.float32).reshape(spans, SPAN, MIXER_HEADS)
    decay_blocks = decay_stream.astype(jnp.float32).reshape(spans, SPAN, MIXER_HEADS)
    causal = jnp.arange(SPAN)[:, None] >= jnp.arange(SPAN)[None, :]

    def step(state, block):
        x_one, b_one, c_one, dt_one, decay_one = block
        running = jnp.cumsum(decay_one, axis=0)
        scores = jnp.einsum('tgn,sgn->gts', c_one.astype(jnp.float32), b_one.astype(jnp.float32))
        gap = running.T[:, :, None] - running.T[:, None, :]
        decay_matrix = jnp.where(causal, jnp.exp(jnp.where(causal, gap, 0.0)), 0.0) * dt_one.T[:, None, :]
        weights = (decay_matrix.reshape(GROUPS, per_group, SPAN, SPAN) * scores[:, None]).astype(jnp.bfloat16)
        intra = jnp.einsum('gkts,sgkp->tgkp', weights.astype(jnp.float32), x_one.astype(jnp.float32))
        tail = jnp.exp(running[-1:] - running) * dt_one
        weighted_input = (x_one.astype(jnp.float32) * tail.reshape(SPAN, GROUPS, per_group, 1)).astype(jnp.bfloat16)
        fresh = jnp.einsum('sgkp,sgn->gkpn', weighted_input.astype(jnp.float32), b_one.astype(jnp.float32))
        inter = jnp.einsum('tgn,gkpn->tgkp', c_one.astype(jnp.float32), state, precision=lax.Precision.HIGHEST)
        inter = inter * jnp.exp(running).reshape(SPAN, GROUPS, per_group, 1)
        out = intra + inter + skip_gain.reshape(1, GROUPS, per_group, 1) * x_one.astype(jnp.float32)
        new_state = jnp.exp(running[-1]).reshape(GROUPS, per_group, 1, 1) * state + fresh
        return (new_state, out.astype(jnp.bfloat16))
    initial = jnp.zeros((GROUPS, per_group, HEAD_DIM, STATE), jnp.float32)
    _, outputs = lax.scan(step, initial, (x_blocks, b_blocks, c_blocks, dt_blocks, decay_blocks))
    values = outputs.reshape(SEQUENCE_TOKENS, MIXER_HEADS * HEAD_DIM)
    return gated_norm(values, z_stream, norm_gain, per_group * HEAD_DIM)
```

```python
import functools

import jax
import jax.numpy as jnp
from jax import lax
from jax.experimental import pallas as pl
from jax.experimental.pallas import tpu as pltpu
from jax.sharding import Mesh
from jax.sharding import PartitionSpec as P

HEADS = 128
HEAD_DIM = 64
STATE = 128
GROUPS = 8
SPAN = 128
CORES = 2
RING = 8
PEERS = CORES * RING
ROWS = 32
TOKENS = PEERS * ROWS
SPANS = TOKENS // SPAN
FROM = SPAN // ROWS
MINE = HEADS // PEERS
WIDE = MINE * HEAD_DIM
TILES = WIDE // 128
RUNS = 32
PACK = ROWS * (TILES + 2) + 2 * MINE
CUT = STATE * TILES // RUNS
F32 = jnp.float32
BF16 = jnp.bfloat16
VMEM_LIMIT = 24 * 1024 * 1024


def call(body, outs, flops, moved, scratch=()):
    return pl.pallas_call(
        body,
        out_shape=outs,
        scratch_shapes=list(scratch),
        compiler_params=pltpu.CompilerParams(vmem_limit_bytes=VMEM_LIMIT),
        cost_estimate=pl.CostEstimate(flops=flops, bytes_accessed=moved, transcendentals=0),
    )


def like(shape, dtype):
    return jax.ShapeDtypeStruct(shape, dtype)


def silu(x):
    return x / (1.0 + jnp.exp(-x))


def pack_kernel(x_ref, b_ref, c_ref, dt_ref, decay_ref, out_ref):
    steps = jnp.transpose(dt_ref[...].astype(F32))
    decays = jnp.transpose(decay_ref[...].astype(F32))
    for core in range(CORES):
        for ring in range(RING):
            peer = core * RING + ring
            for tile in range(TILES):
                column = ring * CORES * WIDE + core * WIDE + tile * 128
                out_ref[peer, tile * ROWS : (tile + 1) * ROWS, :] = x_ref[:, column : column + 128]
            at = TILES * ROWS
            out_ref[peer, at : at + ROWS, :] = b_ref[:, ring * 128 : (ring + 1) * 128]
            out_ref[peer, at + ROWS : at + 2 * ROWS, :] = c_ref[:, ring * 128 : (ring + 1) * 128]
            head = (ring * CORES + core) * MINE
            both = jnp.concatenate([steps[head : head + MINE], decays[head : head + MINE]], 0)
            both = jnp.concatenate([both, jnp.zeros((2 * MINE, 128 - ROWS), F32)], 1)
            out_ref[peer, at + 2 * ROWS :, :] = both.astype(BF16)


def raw(r_ref, span, tile):
    return r_ref[span * FROM : (span + 1) * FROM, tile * ROWS : (tile + 1) * ROWS, :].reshape(SPAN, 128)


def conv_silu(r_ref, halo_ref, taps_ref, pad_ref, span, tile):
    lanes = slice(tile * 128, (tile + 1) * 128)
    if span == 0:
        pad_ref[0:8, :] = halo_ref[tile].astype(F32)
    else:
        pad_ref[0:8, :] = r_ref[span * FROM - 1, (tile + 1) * ROWS - 16 : (tile + 1) * ROWS, :].astype(F32)[8:16]
    pad_ref[8 : 8 + SPAN, :] = raw(r_ref, span, tile).astype(F32)
    total = pad_ref[5 : 5 + SPAN, :] * taps_ref[0:1, lanes]
    for tap in range(1, 4):
        total = total + pad_ref[5 + tap : 5 + tap + SPAN, :] * taps_ref[tap : tap + 1, lanes]
    return silu(total).astype(BF16)


def decays_of(r_ref, span):
    at = (TILES + 2) * ROWS
    both = jnp.concatenate([r_ref[span * FROM + m, at : at + 2 * MINE, 0:ROWS] for m in range(FROM)], 1)
    both = both.astype(F32)
    steps, decays = both[0:MINE], both[MINE : 2 * MINE]
    row = lax.broadcasted_iota(jnp.int32, (SPAN, SPAN), 0)
    column = lax.broadcasted_iota(jnp.int32, (SPAN, SPAN), 1)
    lower = (row >= column).astype(F32).astype(BF16)
    same = (row == column).astype(F32).astype(BF16)
    upper = (row <= column).astype(F32).astype(BF16)
    last = (((1,), (1,)), ((), ()))
    running = lax.dot_general(lower, decays.astype(BF16), last, preferred_element_type=F32)
    steps_column = lax.dot_general(same, steps.astype(BF16), last, preferred_element_type=F32)
    running_row = jnp.dot(decays.astype(BF16), upper, preferred_element_type=F32)
    return running, steps_column, running_row, steps


def spread(per_head, tile):
    low = lax.broadcasted_iota(jnp.int32, (per_head.shape[0], 128), 1) < HEAD_DIM
    return jnp.where(low, per_head[:, 2 * tile : 2 * tile + 1], per_head[:, 2 * tile + 1 : 2 * tile + 2])


def span_state(r_ref, halo_ref, taps_ref, pad_ref, span):
    running, steps, _, _ = decays_of(r_ref, span)
    tail = jnp.exp(running[SPAN - 1 : SPAN] - running) * steps
    b_conv = conv_silu(r_ref, halo_ref, taps_ref, pad_ref, span, TILES)
    parts, weighted = [], []
    for tile in range(TILES):
        part = conv_silu(r_ref, halo_ref, taps_ref, pad_ref, span, tile)
        parts.append(part)
        weighted.append((part.astype(F32) * spread(tail, tile)).astype(BF16))
    fresh = jnp.dot(
        jnp.transpose(b_conv.astype(F32)).astype(BF16),
        jnp.concatenate(weighted, 1),
        preferred_element_type=F32,
    )
    return jnp.concatenate(parts, 1), b_conv, fresh


def later_kernel(r_ref, taps_ref, x_ref, b_ref, fresh_ref, pad_ref):
    for span in range(1, SPANS):
        x_conv, b_conv, fresh = span_state(r_ref, None, taps_ref, pad_ref, span)
        x_ref[span - 1] = x_conv
        b_ref[span - 1] = b_conv
        fresh_ref[span - 1] = fresh


def first_kernel(r_ref, halo_ref, taps_ref, fresh_ref, x_ref, b_ref, own_ref, message_ref, pad_ref):
    x_conv, b_conv, state = span_state(r_ref, halo_ref, taps_ref, pad_ref, 0)
    x_ref[...] = x_conv
    b_ref[...] = b_conv
    own_ref[...] = state
    totals = [decays_of(r_ref, span)[0][SPAN - 1 : SPAN] for span in range(SPANS)]
    factor = jnp.exp(sum(totals[1:], totals[0]))
    for tile in range(TILES):
        lanes = slice(tile * 128, (tile + 1) * 128)
        here = state[:, lanes]
        for span in range(1, SPANS):
            here = here * spread(jnp.exp(totals[span]), tile) + fresh_ref[span - 1, :, lanes]
        scale = spread(factor, tile)
        coarse = scale.astype(BF16).astype(F32)
        tail = jnp.concatenate([coarse, scale - coarse, jnp.zeros((6, 128), F32)], 0)
        for cut in range(STATE // CUT):
            whole = jnp.concatenate([here[cut * CUT : (cut + 1) * CUT], tail], 0)
            message_ref[tile * (STATE // CUT) + cut] = whole.astype(BF16)


def local_kernel(
    r_ref, halo_ref, taps_ref, x0_ref, b0_ref, fresh0_ref, x_ref, b_ref, fresh_ref, part_ref, c_ref, scale_ref, pad_ref
):
    row = lax.broadcasted_iota(jnp.int32, (SPAN, SPAN), 0)
    column = lax.broadcasted_iota(jnp.int32, (SPAN, SPAN), 1)
    causal = row >= column
    low = lax.broadcasted_iota(jnp.int32, (SPAN, 128), 1) < HEAD_DIM
    before = jnp.zeros((1, MINE), F32)
    state = None
    for span in range(SPANS):
        running, _, running_row, steps_row = decays_of(r_ref, span)
        c_conv = conv_silu(r_ref, halo_ref, taps_ref, pad_ref, span, TILES + 1)
        c_ref[span] = c_conv
        x_conv = x0_ref[...] if span == 0 else x_ref[span - 1]
        b_conv = b0_ref[...] if span == 0 else b_ref[span - 1]
        scores = lax.dot_general(c_conv, b_conv, (((1,), (1,)), ((), ())), preferred_element_type=F32)
        grown = jnp.exp(running)
        scale_ref[span] = jnp.exp(running + before)
        for tile in range(TILES):
            lanes = slice(tile * 128, (tile + 1) * 128)
            pair = []
            for head in (2 * tile, 2 * tile + 1):
                gap = running[:, head : head + 1] - running_row[head : head + 1, :]
                decay = jnp.exp(jnp.where(causal, gap, -1e30)) * steps_row[head : head + 1, :]
                pair.append((decay * scores).astype(BF16))
            values = x_conv[:, lanes]
            both = jnp.dot(jnp.concatenate(pair, 0), values, preferred_element_type=F32)
            out = jnp.where(low, both[:SPAN], both[SPAN:])
            out = out + values.astype(F32) * taps_ref[4:5, lanes]
            if span:
                inter = jnp.dot(c_conv, state[:, lanes].astype(BF16), preferred_element_type=F32)
                out = out + inter * spread(grown, tile)
            part_ref[span, :, lanes] = out
        total = running[SPAN - 1 : SPAN]
        before = before + total
        if span == 0:
            state = fresh0_ref[...]
        elif span < SPANS - 1:
            factor = jnp.exp(total)
            kept = [state[:, t * 128 : (t + 1) * 128] * spread(factor, t) for t in range(TILES)]
            state = jnp.concatenate(kept, 1) + fresh_ref[span - 1]


def chain_kernel(all_ref, out_ref):
    state = jnp.zeros((CUT, 128), F32)
    for run in range(RUNS):
        out_ref[run] = state.astype(BF16)
        if run < RUNS - 1:
            here = all_ref[run].astype(F32)
            state = state * (here[CUT : CUT + 1] + here[CUT + 1 : CUT + 2]) + here[:CUT]


def finish_kernel(part_ref, c_ref, scale_ref, state_ref, out_ref):
    for span in range(SPANS):
        scale = scale_ref[span]
        for tile in range(TILES):
            lanes = slice(tile * 128, (tile + 1) * 128)
            inter = jnp.dot(c_ref[span], state_ref[tile], preferred_element_type=F32)
            out = part_ref[span, :, lanes] + inter * spread(scale, tile)
            out_ref[span * SPAN : (span + 1) * SPAN, lanes] = out.astype(BF16)


def norm_kernel(values_ref, z_ref, gain_ref, out_ref):
    for group in range(GROUPS):
        gated, square = [], None
        for core in range(CORES):
            lanes = slice((group * CORES + core) * WIDE, (group * CORES + core + 1) * WIDE)
            here = values_ref[core * RING + group].astype(F32) * silu(z_ref[:, lanes].astype(F32))
            gated.append((lanes, here))
            summed = jnp.sum(here * here, axis=1, keepdims=True)
            square = summed if square is None else square + summed
        scale = lax.rsqrt(square * (1.0 / (CORES * WIDE)) + 1e-05)
        for lanes, here in gated:
            out_ref[:, lanes] = (here * scale * gain_ref[:, lanes].astype(F32)).astype(BF16)


def shards(
    x_stream,
    z_stream,
    b_stream,
    c_stream,
    dt_stream,
    decay_stream,
    kernel_x,
    kernel_b,
    kernel_c,
    skip_gain,
    norm_gain,
):
    core = lax.axis_index("core")
    packed = call(pack_kernel, like((PEERS, PACK, 128), BF16), 0, 2 * PEERS * PACK * 256)(
        x_stream, b_stream, c_stream, dt_stream, decay_stream
    )
    got = lax.all_to_all(packed, ("core", "head"), split_axis=0, concat_axis=0, tiled=True)
    edge = got[PEERS - 1, : ROWS * (TILES + 2)].reshape(TILES + 2, ROWS, 128)[:, ROWS - 8 :]
    halo = lax.ppermute(edge, "seq", [(i, i + 1) for i in range(RUNS - 1)])
    taps_x = lax.dynamic_slice_in_dim(kernel_x, core * WIDE, WIDE, 1)
    skip = jnp.repeat(lax.dynamic_slice_in_dim(skip_gain, core * MINE, MINE), HEAD_DIM)
    taps = jnp.concatenate([taps_x, kernel_b, kernel_c], 1).astype(F32)
    skip_row = jnp.pad(skip, (0, 2 * STATE))[None]
    taps = jnp.concatenate([taps, skip_row, jnp.zeros((3, WIDE + 2 * STATE), F32)], 0)
    pad = pltpu.VMEM((SPAN + 8, 128), F32)
    x_later, b_later, fresh_later = call(
        later_kernel,
        (
            like((SPANS - 1, SPAN, WIDE), BF16),
            like((SPANS - 1, SPAN, STATE), BF16),
            like((SPANS - 1, STATE, WIDE), F32),
        ),
        10**9,
        4 * 10**6,
        [pad],
    )(got, taps)
    x_first, b_first, fresh_first, message = call(
        first_kernel,
        (
            like((SPAN, WIDE), BF16),
            like((SPAN, STATE), BF16),
            like((STATE, WIDE), F32),
            like((RUNS, CUT + 8, 128), BF16),
        ),
        10**9,
        4 * 10**6,
        [pad],
    )(got, halo, taps, fresh_later)
    slices = lax.all_to_all(message, "seq", split_axis=0, concat_axis=0, tiled=True)
    part, c_conv, scale = call(
        local_kernel,
        (
            like((SPANS, SPAN, WIDE), F32),
            like((SPANS, SPAN, STATE), BF16),
            like((SPANS, SPAN, MINE), F32),
        ),
        10**9,
        8 * 10**6,
        [pad],
    )(got, halo, taps, x_first, b_first, fresh_first, x_later, b_later, fresh_later)
    chained = call(chain_kernel, like((RUNS, CUT, 128), BF16), 10**7, 10**6)(slices)
    state = lax.all_to_all(chained, "seq", split_axis=0, concat_axis=0, tiled=True)
    values = call(finish_kernel, like((TOKENS, WIDE), BF16), 10**8, 3 * 10**6)(
        part, c_conv, scale, state.reshape(TILES, STATE, 128)
    )
    home = lax.all_to_all(
        values.reshape(PEERS, ROWS, WIDE), ("core", "head"), split_axis=0, concat_axis=0, tiled=True
    )
    return call(norm_kernel, like((ROWS, HEADS * HEAD_DIM), BF16), 10**7, 2 * 10**6)(
        home, z_stream, norm_gain.reshape(1, HEADS * HEAD_DIM)
    )


def solution(mesh):
    finer = Mesh(mesh.devices.reshape(RUNS, CORES, RING), ("seq", "core", "head"))
    rows = P(("seq", "core", "head"), None)
    in_specs = (rows,) * 6 + (P(None, "head"),) * 3 + (P("head"), P())
    return jax.shard_map(shards, mesh=finer, in_specs=in_specs, out_specs=rows, check_vma=False)
```

```python
import functools

import jax
import jax.numpy as jnp
from jax import lax
from jax.experimental import pallas as pl
from jax.experimental.pallas import tpu as pltpu
from jax.sharding import Mesh
from jax.sharding import PartitionSpec as P

HEADS = 128
HEAD_DIM = 64
STATE = 128
GROUPS = 8
SPAN = 128
CORES = 2
RING = 8
PEERS = CORES * RING
ROWS = 32
TOKENS = PEERS * ROWS
SPANS = TOKENS // SPAN
FROM = SPAN // ROWS
MINE = HEADS // PEERS
WIDE = MINE * HEAD_DIM
TILES = WIDE // 128
LEADERS = 4
MEMBERS = PEERS // LEADERS
RIM = 8 * (TILES + 2)
RUNS = 32
PACK = ROWS * (TILES + 2) + MINE
CUT = STATE * TILES // RUNS
F32 = jnp.float32
BF16 = jnp.bfloat16
MIB = 1024 * 1024


def call(body, outs, flops, moved, scratch=(), vmem=16, **specs):
    return pl.pallas_call(
        body,
        **specs,
        out_shape=outs,
        scratch_shapes=list(scratch),
        compiler_params=pltpu.CompilerParams(vmem_limit_bytes=vmem * MIB),
        cost_estimate=pl.CostEstimate(flops=flops, bytes_accessed=moved, transcendentals=0),
    )


def like(shape, dtype):
    return jax.ShapeDtypeStruct(shape, dtype)


def silu(x):
    return x / (1.0 + jnp.exp(-x))


def pack_kernel(x_hbm, b_hbm, c_hbm, dt_hbm, decay_hbm, out_ref, *rest):
    rims, (x_ref, b_ref, c_ref, dt_ref, decay_ref, arrived) = rest[:LEADERS], rest[LEADERS:]
    pairs = ((dt_hbm, dt_ref), (decay_hbm, decay_ref), (b_hbm, b_ref), (c_hbm, c_ref), (x_hbm, x_ref))
    copies = [pltpu.make_async_copy(a, b, arrived.at[i]) for i, (a, b) in enumerate(pairs)]
    for copy in copies:
        copy.start()
    copies[0].wait()
    copies[1].wait()
    steps = jnp.transpose(dt_ref[...].astype(F32))
    decays = jnp.transpose(decay_ref[...].astype(F32))
    at = TILES * ROWS
    for copy in copies[2:4]:
        copy.wait()
    for core in range(CORES):
        for ring in range(RING):
            peer = core * RING + ring
            out_ref[peer, at : at + ROWS, :] = b_ref[:, ring * 128 : (ring + 1) * 128]
            out_ref[peer, at + ROWS : at + 2 * ROWS, :] = c_ref[:, ring * 128 : (ring + 1) * 128]
            head = (ring * CORES + core) * MINE
            rest = jnp.zeros((MINE, 128 - 2 * ROWS), F32)
            both = jnp.concatenate([steps[head : head + MINE], decays[head : head + MINE], rest], 1)
            out_ref[peer, at + 2 * ROWS :, :] = both.astype(BF16)
    copies[4].wait()
    for core in range(CORES):
        for ring in range(RING):
            for tile in range(TILES):
                column = ring * CORES * WIDE + core * WIDE + tile * 128
                out_ref[core * RING + ring, tile * ROWS : (tile + 1) * ROWS, :] = x_ref[:, column : column + 128]
    for leader in range(LEADERS):
        for member in range(MEMBERS):
            core, ring = divmod(leader * MEMBERS + member, RING)
            column = (ring * CORES + core) * WIDE
            rows = slice(ROWS - 16, ROWS)
            pieces = [x_ref[rows, column + tile * 128 : column + (tile + 1) * 128] for tile in range(TILES)]
            pieces += [ref[rows, ring * 128 : (ring + 1) * 128] for ref in (b_ref, c_ref)]
            whole = jnp.concatenate([piece.astype(F32)[8:] for piece in pieces], 0)
            rims[leader][member] = whole.astype(BF16)


def raw(r_ref, span, tile):
    return r_ref[span * FROM : (span + 1) * FROM, tile * ROWS : (tile + 1) * ROWS, :].reshape(SPAN, 128)


def conv_silu(r_ref, rim_ref, taps_ref, pad_ref, span, tile):
    lanes = slice(tile * 128, (tile + 1) * 128)
    if span == 0:
        pad_ref[0:8, :] = rim_ref[tile * 8 : (tile + 1) * 8]
    else:
        pad_ref[0:8, :] = r_ref[span * FROM - 1, (tile + 1) * ROWS - 16 : (tile + 1) * ROWS, :].astype(F32)[8:16]
    pad_ref[8 : 8 + SPAN, :] = raw(r_ref, span, tile).astype(F32)
    total = pad_ref[5 : 5 + SPAN, :] * taps_ref[0:1, lanes]
    for tap in range(1, 4):
        total = total + pad_ref[5 + tap : 5 + tap + SPAN, :] * taps_ref[tap : tap + 1, lanes]
    return silu(total).astype(BF16)


def decays_of(r_ref, span):
    at = (TILES + 2) * ROWS
    parts = [r_ref[span * FROM + m, at : at + MINE, :].astype(F32) for m in range(FROM)]
    steps = jnp.concatenate([part[:, :ROWS] for part in parts], 1)
    decays = jnp.concatenate([part[:, ROWS : 2 * ROWS] for part in parts], 1)
    row = lax.broadcasted_iota(jnp.int32, (SPAN, SPAN), 0)
    column = lax.broadcasted_iota(jnp.int32, (SPAN, SPAN), 1)
    lower = (row >= column).astype(F32).astype(BF16)
    same = (row == column).astype(F32).astype(BF16)
    upper = (row <= column).astype(F32).astype(BF16)
    last = (((1,), (1,)), ((), ()))
    running = lax.dot_general(lower, decays.astype(BF16), last, preferred_element_type=F32)
    steps_column = lax.dot_general(same, steps.astype(BF16), last, preferred_element_type=F32)
    running_row = jnp.dot(decays.astype(BF16), upper, preferred_element_type=F32)
    return running, steps_column, running_row, steps


def spread(per_head, tile):
    low = lax.broadcasted_iota(jnp.int32, (per_head.shape[0], 128), 1) < HEAD_DIM
    return jnp.where(low, per_head[:, 2 * tile : 2 * tile + 1], per_head[:, 2 * tile + 1 : 2 * tile + 2])


def span_state(r_ref, rim_ref, taps_ref, pad_ref, span):
    running, steps, _, _ = decays_of(r_ref, span)
    tail = jnp.exp(running[SPAN - 1 : SPAN] - running) * steps
    b_conv = conv_silu(r_ref, rim_ref, taps_ref, pad_ref, span, TILES)
    parts, weighted = [], []
    for tile in range(TILES):
        part = conv_silu(r_ref, rim_ref, taps_ref, pad_ref, span, tile)
        parts.append(part)
        weighted.append((part.astype(F32) * spread(tail, tile)).astype(BF16))
    fresh = jnp.dot(
        jnp.transpose(b_conv.astype(F32)).astype(BF16),
        jnp.concatenate(weighted, 1),
        preferred_element_type=F32,
    )
    return jnp.concatenate(parts, 1), b_conv, fresh, running


def gather_rim(rims, rim_ref):
    total = rims[0][0].astype(F32)
    for ref in rims[1:]:
        total = total + ref[...].astype(F32)
    rim_ref[...] = total


def state_kernel(r_ref, taps_ref, *rest):
    rims, (message_ref, rim_ref, pad_ref) = rest[:MEMBERS], rest[MEMBERS:]
    gather_rim(rims, rim_ref)
    total, state = None, None
    for span in range(SPANS):
        _, _, fresh, running = span_state(r_ref, rim_ref, taps_ref, pad_ref, span)
        last = running[SPAN - 1 : SPAN]
        if span == 0:
            total, state = last, fresh
        else:
            factor = jnp.exp(last)
            kept = [state[:, t * 128 : (t + 1) * 128] * spread(factor, t) for t in range(TILES)]
            total, state = total + last, jnp.concatenate(kept, 1) + fresh
    factor = jnp.exp(total)
    for tile in range(TILES):
        here = state[:, tile * 128 : (tile + 1) * 128]
        scale = spread(factor, tile)
        coarse = scale.astype(BF16).astype(F32)
        tail = jnp.concatenate([coarse, scale - coarse, jnp.zeros((6, 128), F32)], 0)
        for cut in range(STATE // CUT):
            whole = jnp.concatenate([here[cut * CUT : (cut + 1) * CUT], tail], 0)
            message_ref[tile * (STATE // CUT) + cut] = whole.astype(BF16)


def local_kernel(r_ref, taps_ref, *rest):
    rims, (part_ref, c_ref, scale_ref, rim_ref, pad_ref) = rest[:MEMBERS], rest[MEMBERS:]
    gather_rim(rims, rim_ref)
    row = lax.broadcasted_iota(jnp.int32, (SPAN, SPAN), 0)
    column = lax.broadcasted_iota(jnp.int32, (SPAN, SPAN), 1)
    causal = row >= column
    low = lax.broadcasted_iota(jnp.int32, (SPAN, 128), 1) < HEAD_DIM
    before = jnp.zeros((1, MINE), F32)
    state = None
    for span in range(SPANS):
        running, _, running_row, steps_row = decays_of(r_ref, span)
        c_conv = conv_silu(r_ref, rim_ref, taps_ref, pad_ref, span, TILES + 1)
        c_ref[span] = c_conv
        x_conv, b_conv, fresh, _ = span_state(r_ref, rim_ref, taps_ref, pad_ref, span)
        scores = lax.dot_general(c_conv, b_conv, (((1,), (1,)), ((), ())), preferred_element_type=F32)
        grown = jnp.exp(running)
        scale = jnp.exp(running + before)
        for tile in range(TILES):
            lanes = slice(tile * 128, (tile + 1) * 128)
            pair = []
            for head in (2 * tile, 2 * tile + 1):
                gap = running[:, head : head + 1] - running_row[head : head + 1, :]
                decay = jnp.exp(jnp.where(causal, gap, -1e30)) * steps_row[head : head + 1, :]
                pair.append((decay * scores).astype(BF16))
            values = x_conv[:, lanes]
            both = jnp.dot(jnp.concatenate(pair, 0), values, preferred_element_type=F32)
            out = jnp.where(low, both[:SPAN], both[SPAN:])
            out = out + values.astype(F32) * taps_ref[4:5, lanes]
            if span:
                inter = jnp.dot(c_conv, state[:, lanes].astype(BF16), preferred_element_type=F32)
                out = out + inter * spread(grown, tile)
            part_ref[span, :, lanes] = out
            scale_ref[span, :, lanes] = spread(scale, tile)
        total = running[SPAN - 1 : SPAN]
        before = before + total
        if span == 0:
            state = fresh
        elif span < SPANS - 1:
            factor = jnp.exp(total)
            kept = [state[:, t * 128 : (t + 1) * 128] * spread(factor, t) for t in range(TILES)]
            state = jnp.concatenate(kept, 1) + fresh


def chain_kernel(all_ref, out_ref):
    state = jnp.zeros((CUT, 128), F32)
    for run in range(RUNS):
        out_ref[run] = state.astype(BF16)
        if run < RUNS - 1:
            here = all_ref[run].astype(F32)
            state = state * (here[CUT : CUT + 1] + here[CUT + 1 : CUT + 2]) + here[:CUT]


def finish_kernel(part_ref, c_ref, scale_ref, state_ref, out_ref):
    for span in range(SPANS):
        for tile in range(TILES):
            lanes = slice(tile * 128, (tile + 1) * 128)
            inter = jnp.dot(c_ref[span], state_ref[tile], preferred_element_type=F32)
            out = part_ref[span, :, lanes] + inter * scale_ref[span, :, lanes]
            out_ref[span * SPAN : (span + 1) * SPAN, lanes] = out.astype(BF16)


def norm_kernel(values_ref, z_ref, gain_ref, out_ref):
    for group in range(GROUPS):
        gated, square = [], None
        for core in range(CORES):
            lanes = slice((group * CORES + core) * WIDE, (group * CORES + core + 1) * WIDE)
            here = values_ref[core * RING + group].astype(F32) * silu(z_ref[:, lanes].astype(F32))
            gated.append((lanes, here))
            summed = jnp.sum(here * here, axis=1, keepdims=True)
            square = summed if square is None else square + summed
        scale = lax.rsqrt(square * (1.0 / (CORES * WIDE)) + 1e-05)
        for lanes, here in gated:
            out_ref[:, lanes] = (here * scale * gain_ref[:, lanes].astype(F32)).astype(BF16)


def shards(
    x_stream,
    z_stream,
    b_stream,
    c_stream,
    dt_stream,
    decay_stream,
    kernel_x,
    kernel_b,
    kernel_c,
    skip_gain,
    norm_gain,
):
    core = lax.axis_index("core")
    streams = (x_stream, b_stream, c_stream, dt_stream, decay_stream)
    packed, *rims = call(
        pack_kernel,
        (like((PEERS, PACK, 128), BF16),) + (like((MEMBERS, RIM, 128), BF16),) * LEADERS,
        0,
        2 * PEERS * PACK * 256,
        [pltpu.VMEM(stream.shape, BF16) for stream in streams] + [pltpu.SemaphoreType.DMA((5,))],
        vmem=60,
        in_specs=[pl.BlockSpec(memory_space=pltpu.HBM)] * 5,
    )(*streams)
    got = lax.all_to_all(packed, ("core", "head"), split_axis=0, concat_axis=0, tiled=True)
    everyone = ("seq", "core", "head")
    led = None
    for leader, rim in enumerate(rims):
        pairs = [(i * PEERS + PEERS - 1, (i + 1) * PEERS + leader * MEMBERS) for i in range(RUNS - 1)]
        came = lax.ppermute(rim, everyone, pairs)
        led = came if led is None else led + came
    handed = [led]
    for member in range(1, MEMBERS):
        pairs = [(i, i + member) for i in range(0, RUNS * PEERS, MEMBERS)]
        handed.append(lax.ppermute(led[member], everyone, pairs))
    taps_x = lax.dynamic_slice_in_dim(kernel_x, core * WIDE, WIDE, 1)
    skip = jnp.repeat(lax.dynamic_slice_in_dim(skip_gain, core * MINE, MINE), HEAD_DIM)
    taps = jnp.concatenate([taps_x, kernel_b, kernel_c], 1).astype(F32)
    skip_row = jnp.pad(skip, (0, 2 * STATE))[None]
    taps = jnp.concatenate([taps, skip_row, jnp.zeros((3, WIDE + 2 * STATE), F32)], 0)
    pad = pltpu.VMEM((SPAN + 8, 128), F32)
    rim = pltpu.VMEM((RIM, 128), F32)
    message = call(state_kernel, like((RUNS, CUT + 8, 128), BF16), 10**9, 2 * 10**6, [rim, pad])(got, taps, *handed)
    slices = lax.all_to_all(message, "seq", split_axis=0, concat_axis=0, tiled=True)
    part, c_conv, scale = call(
        local_kernel,
        (
            like((SPANS, SPAN, WIDE), F32),
            like((SPANS, SPAN, STATE), BF16),
            like((SPANS, SPAN, WIDE), F32),
        ),
        10**9,
        8 * 10**6,
        [rim, pad],
    )(got, taps, *handed)
    slices, part = lax.optimization_barrier((slices, part))
    chained = call(chain_kernel, like((RUNS, CUT, 128), BF16), 10**7, 10**6)(slices)
    state = lax.all_to_all(chained, "seq", split_axis=0, concat_axis=0, tiled=True)
    values = call(finish_kernel, like((TOKENS, WIDE), BF16), 10**8, 3 * 10**6)(
        part, c_conv, scale, state.reshape(TILES, STATE, 128)
    )
    home = lax.all_to_all(
        values.reshape(PEERS, ROWS, WIDE), ("core", "head"), split_axis=0, concat_axis=0, tiled=True
    )
    return call(norm_kernel, like((ROWS, HEADS * HEAD_DIM), BF16), 10**7, 2 * 10**6)(
        home, z_stream, norm_gain.reshape(1, HEADS * HEAD_DIM)
    )


def solution(mesh):
    finer = Mesh(mesh.devices.reshape(RUNS, CORES, RING), ("seq", "core", "head"))
    rows = P(("seq", "core", "head"), None)
    in_specs = (rows,) * 6 + (P(None, "head"),) * 3 + (P("head"), P())
    return jax.shard_map(shards, mesh=finer, in_specs=in_specs, out_specs=rows, check_vma=False)
```

```python
import functools

import jax
import jax.numpy as jnp
from jax import lax
from jax.experimental import pallas as pl
from jax.experimental.pallas import tpu as pltpu
from jax.sharding import Mesh
from jax.sharding import PartitionSpec as P

HEADS = 128
HEAD_DIM = 64
STATE = 128
GROUPS = 8
SPAN = 128
CORES = 2
RING = 8
PEERS = CORES * RING
ROWS = 32
TOKENS = PEERS * ROWS
SPANS = TOKENS // SPAN
FROM = SPAN // ROWS
MINE = HEADS // PEERS
WIDE = MINE * HEAD_DIM
TILES = WIDE // 128
LEADERS = 4
MEMBERS = PEERS // LEADERS
RIM = 8 * (TILES + 2)
RUNS = 32
HALF = ROWS // CORES
PACK = ROWS * (TILES + 1) + HALF + MINE
CUT = STATE * TILES // RUNS
F32 = jnp.float32
BF16 = jnp.bfloat16
MIB = 1024 * 1024


def call(body, outs, flops, moved, scratch=(), vmem=16, **specs):
    return pl.pallas_call(
        body,
        **specs,
        out_shape=outs,
        scratch_shapes=list(scratch),
        compiler_params=pltpu.CompilerParams(vmem_limit_bytes=vmem * MIB),
        cost_estimate=pl.CostEstimate(flops=flops, bytes_accessed=moved, transcendentals=0),
    )


def like(shape, dtype):
    return jax.ShapeDtypeStruct(shape, dtype)


def silu(x):
    half = 0.5 * x
    return half * jnp.tanh(half) + half


def pack_kernel(x_hbm, b_hbm, c_hbm, dt_hbm, decay_hbm, out_ref, *rest):
    rims, (x_ref, b_ref, c_ref, dt_ref, decay_ref, arrived) = rest[:LEADERS], rest[LEADERS:]
    pairs = ((dt_hbm, dt_ref), (decay_hbm, decay_ref), (b_hbm, b_ref), (c_hbm, c_ref), (x_hbm, x_ref))
    copies = [pltpu.make_async_copy(a, b, arrived.at[i]) for i, (a, b) in enumerate(pairs)]
    for copy in copies:
        copy.start()
    copies[0].wait()
    copies[1].wait()
    steps = jnp.transpose(dt_ref[...].astype(F32))
    decays = jnp.transpose(decay_ref[...].astype(F32))
    at = TILES * ROWS
    for copy in copies[2:4]:
        copy.wait()
    for core in range(CORES):
        for ring in range(RING):
            peer = core * RING + ring
            out_ref[peer, at : at + ROWS, :] = b_ref[:, ring * 128 : (ring + 1) * 128]
            rows = slice(core * HALF, (core + 1) * HALF)
            out_ref[peer, at + ROWS : at + ROWS + HALF, :] = c_ref[rows, ring * 128 : (ring + 1) * 128]
            head = (ring * CORES + core) * MINE
            rest = jnp.zeros((MINE, 128 - 2 * ROWS), F32)
            both = jnp.concatenate([steps[head : head + MINE], decays[head : head + MINE], rest], 1)
            out_ref[peer, at + ROWS + HALF :, :] = both.astype(BF16)
    copies[4].wait()
    for core in range(CORES):
        for ring in range(RING):
            for tile in range(TILES):
                column = ring * CORES * WIDE + core * WIDE + tile * 128
                out_ref[core * RING + ring, tile * ROWS : (tile + 1) * ROWS, :] = x_ref[:, column : column + 128]
    for leader in range(LEADERS):
        for member in range(MEMBERS):
            core, ring = divmod(leader * MEMBERS + member, RING)
            column = (ring * CORES + core) * WIDE
            rows = slice(ROWS - 16, ROWS)
            pieces = [x_ref[rows, column + tile * 128 : column + (tile + 1) * 128] for tile in range(TILES)]
            pieces += [ref[rows, ring * 128 : (ring + 1) * 128] for ref in (b_ref, c_ref)]
            whole = jnp.concatenate([piece.astype(F32)[8:] for piece in pieces], 0)
            rims[leader][member] = whole.astype(BF16)


def raw(r_ref, span, tile):
    return r_ref[span * FROM : (span + 1) * FROM, tile * ROWS : (tile + 1) * ROWS, :].reshape(SPAN, 128)


def c_rows(r_ref):
    at = (TILES + 1) * ROWS
    return r_ref[:, at : at + HALF, :]


def fill(r_ref, rims, pad_ref, tiles):
    for tile in tiles:
        rows = slice(tile * 8, (tile + 1) * 8)
        edge = rims[0][0, rows, :].astype(F32)
        for ref in rims[1:]:
            edge = edge + ref[rows, :].astype(F32)
        pad_ref[tile, 0:8, :] = edge
        if tile > TILES:
            continue
        for span in range(SPANS):
            pad_ref[tile, 8 + span * SPAN : 8 + (span + 1) * SPAN, :] = raw(r_ref, span, tile).astype(F32)


def conv_silu(taps_ref, pad_ref, span, tile):
    lanes = slice(tile * 128, (tile + 1) * 128)
    at = span * SPAN
    whole = pad_ref[tile, at : at + SPAN + 8, :]
    total = whole[8:] * taps_ref[3:4, lanes]
    for tap in range(3):
        total = total + pltpu.roll(whole, 3 - tap, 0)[8:] * taps_ref[tap : tap + 1, lanes]
    return silu(total).astype(BF16)


def rows_of(r_ref):
    at = (TILES + 1) * ROWS + HALF
    steps, decays = [], []
    for span in range(SPANS):
        parts = [r_ref[span * FROM + m, at : at + MINE, :].astype(F32) for m in range(FROM)]
        steps.append(jnp.concatenate([part[:, :ROWS] for part in parts], 1))
        decays.append(jnp.concatenate([part[:, ROWS : 2 * ROWS] for part in parts], 1))
    decays = jnp.concatenate(decays, 0)
    row = lax.broadcasted_iota(jnp.int32, (SPAN, SPAN), 0)
    column = lax.broadcasted_iota(jnp.int32, (SPAN, SPAN), 1)
    upper = (row <= column).astype(F32).astype(BF16)
    running = jnp.dot(decays.astype(BF16), upper, preferred_element_type=F32)
    return jnp.concatenate(steps, 0), running


def terms(x, count):
    parts = []
    for _ in range(count):
        parts.append(x.astype(BF16))
        x = x - parts[-1].astype(F32)
    return parts


def own_lanes(count):
    row = lax.broadcasted_iota(jnp.int32, (count * MINE, WIDE), 0)
    column = lax.broadcasted_iota(jnp.int32, (count * MINE, WIDE), 1)
    return (lax.rem(row, MINE) == lax.div(column, HEAD_DIM)).astype(F32).astype(BF16)


def widen(per_head, lanes, count):
    stack = jnp.concatenate([part.astype(F32) for part in terms(per_head, count)], 0).astype(BF16)
    return lax.dot_general(stack, lanes, (((0,), (0,)), ((), ())), preferred_element_type=F32)


def span_state(taps_ref, pad_ref, span, tail):
    b_conv = conv_silu(taps_ref, pad_ref, span, TILES)
    parts = [conv_silu(taps_ref, pad_ref, span, tile) for tile in range(TILES)]
    x_conv = jnp.concatenate(parts, 1)
    weighted = (x_conv.astype(F32) * tail).astype(BF16)
    b_turned = jnp.transpose(b_conv.astype(F32)).astype(BF16)
    return x_conv, b_conv, jnp.dot(b_turned, weighted, preferred_element_type=F32)


def of_span(x, span):
    return x[span * MINE : (span + 1) * MINE]


def state_kernel(r_ref, taps_ref, *rest):
    rims, (message_ref, half_ref, pad_ref) = rest[:MEMBERS], rest[MEMBERS:]
    half_ref[...] = c_rows(r_ref)
    fill(r_ref, rims, pad_ref, range(TILES + 1))
    steps, running = rows_of(r_ref)
    lanes = own_lanes(2)
    tails = jnp.exp(running[:, SPAN - 1 :] - running) * steps
    last = [of_span(running, span)[:, SPAN - 1 :] for span in range(SPANS)]
    factors = jnp.exp(jnp.concatenate(last + [last[0] + last[1] + last[2] + last[3]], 1))
    factors = jnp.concatenate([factors, jnp.zeros((MINE, SPAN - SPANS - 1), F32)], 1)
    factors = widen(factors, lanes, 2)
    state = None
    for span in range(SPANS):
        _, _, fresh = span_state(taps_ref, pad_ref, span, widen(of_span(tails, span), lanes, 2))
        state = fresh if span == 0 else state * factors[span : span + 1] + fresh
    scale = factors[SPANS : SPANS + 1]
    coarse = scale.astype(BF16).astype(F32)
    tail = jnp.concatenate([coarse, scale - coarse, jnp.zeros((6, WIDE), F32)], 0)
    for tile in range(TILES):
        here = slice(tile * 128, (tile + 1) * 128)
        for cut in range(STATE // CUT):
            whole = jnp.concatenate([state[cut * CUT : (cut + 1) * CUT, here], tail[:, here]], 0)
            message_ref[tile * (STATE // CUT) + cut] = whole.astype(BF16)


def local_kernel(core_ref, r_ref, other_ref, taps_ref, *rest):
    rims, (part_ref, c_ref, scale_ref, pad_ref) = rest[:MEMBERS], rest[MEMBERS:]
    fill(r_ref, rims, pad_ref, range(TILES + 2))
    first = core_ref[0] == 0
    own, other = c_rows(r_ref).astype(F32), other_ref[...].astype(F32)
    whole = jnp.concatenate([jnp.where(first, own, other), jnp.where(first, other, own)], 1)
    pad_ref[TILES + 1, 8:, :] = whole.reshape(TOKENS, 128)
    row = lax.broadcasted_iota(jnp.int32, (SPAN, SPAN), 0)
    column = lax.broadcasted_iota(jnp.int32, (SPAN, SPAN), 1)
    causal = row >= column
    low = lax.broadcasted_iota(jnp.int32, (SPAN, 128), 1) < HEAD_DIM
    steps, running = rows_of(r_ref)
    lanes_two, lanes_three = own_lanes(2), own_lanes(3)
    tails = jnp.exp(running[:, SPAN - 1 :] - running) * steps
    turned = jnp.transpose(jnp.concatenate([running, jnp.zeros((SPAN - SPANS * MINE, SPAN), F32)], 0))
    before = jnp.zeros((MINE, 1), F32)
    state = None
    for span in range(SPANS):
        c_conv = conv_silu(taps_ref, pad_ref, span, TILES + 1)
        c_ref[span] = c_conv
        x_conv, b_conv, fresh = span_state(taps_ref, pad_ref, span, widen(of_span(tails, span), lanes_two, 2))
        scores = lax.dot_general(c_conv, b_conv, (((1,), (1,)), ((), ())), preferred_element_type=F32)
        here = of_span(running, span)
        grown = widen(jnp.exp(here), lanes_two, 2)
        scale_ref[span] = grown if span == 0 else widen(jnp.exp(here + before), lanes_two, 2)
        outs = []
        for tile in range(TILES):
            lanes = slice(tile * 128, (tile + 1) * 128)
            pair = []
            for head in (2 * tile, 2 * tile + 1):
                at = span * MINE + head
                gap = turned[:, at : at + 1] - running[at : at + 1]
                decay = jnp.exp(jnp.where(causal, gap, -1e30)) * steps[at : at + 1]
                pair.append((decay * scores).astype(BF16))
            both = jnp.dot(jnp.concatenate(pair, 0), x_conv[:, lanes], preferred_element_type=F32)
            outs.append(jnp.where(low, both[:SPAN], both[SPAN:]))
        out = jnp.concatenate(outs, 1) + x_conv.astype(F32) * taps_ref[4:5, :WIDE]
        if span:
            out = out + jnp.dot(c_conv, state.astype(BF16), preferred_element_type=F32) * grown
        part_ref[span] = out
        before = before + here[:, SPAN - 1 :]
        if span == 0:
            state = fresh
        elif span < SPANS - 1:
            state = state * grown[SPAN - 1 :] + fresh


def chain_kernel(all_ref, out_ref):
    state = jnp.zeros((CUT, 128), F32)
    for run in range(RUNS):
        out_ref[run] = state.astype(BF16)
        if run < RUNS - 1:
            here = all_ref[run].astype(F32)
            state = state * (here[CUT : CUT + 1] + here[CUT + 1 : CUT + 2]) + here[:CUT]


def finish_kernel(part_ref, c_ref, scale_ref, state_ref, out_hbm, out_ref, sent):
    state = jnp.concatenate([state_ref[tile] for tile in range(TILES)], 1)
    copies = []
    for span in range(SPANS):
        rows = slice(span * SPAN, (span + 1) * SPAN)
        inter = jnp.dot(c_ref[span], state, preferred_element_type=F32)
        out_ref[rows, :] = (part_ref[span] + inter * scale_ref[span]).astype(BF16)
        copies.append(pltpu.make_async_copy(out_ref.at[rows, :], out_hbm.at[rows, :], sent.at[span]))
        copies[-1].start()
    for copy in copies:
        copy.wait()


def gate_kernel(z_ref, out_ref):
    out_ref[...] = silu(z_ref[...].astype(F32))


def norm_kernel(values_ref, gate_ref, gain_ref, out_hbm, out_ref, sent):
    copies = []
    for group in range(GROUPS):
        whole = slice(group * CORES * WIDE, (group + 1) * CORES * WIDE)
        here = jnp.concatenate([values_ref[core * RING + group] for core in range(CORES)], 1)
        here = here.astype(F32) * gate_ref[:, whole]
        square = jnp.sum(here * here, axis=1, keepdims=True)
        scale = lax.rsqrt(square * (1.0 / (CORES * WIDE)) + 1e-05)
        out_ref[:, whole] = (here * scale * gain_ref[:, whole].astype(F32)).astype(BF16)
        copies.append(pltpu.make_async_copy(out_ref.at[:, whole], out_hbm.at[:, whole], sent.at[group]))
        copies[-1].start()
    for copy in copies:
        copy.wait()


def shards(
    x_stream,
    z_stream,
    b_stream,
    c_stream,
    dt_stream,
    decay_stream,
    kernel_x,
    kernel_b,
    kernel_c,
    skip_gain,
    norm_gain,
):
    core = lax.axis_index("core")
    streams = (x_stream, b_stream, c_stream, dt_stream, decay_stream)
    packed, *rims = call(
        pack_kernel,
        (like((PEERS, PACK, 128), BF16),) + (like((MEMBERS, RIM, 128), BF16),) * LEADERS,
        0,
        2 * PEERS * PACK * 256,
        [pltpu.VMEM(stream.shape, BF16) for stream in streams] + [pltpu.SemaphoreType.DMA((5,))],
        vmem=60,
        in_specs=[pl.BlockSpec(memory_space=pltpu.HBM)] * 5,
    )(*streams)
    got = lax.all_to_all(packed, ("core", "head"), split_axis=0, concat_axis=0, tiled=True)
    everyone = ("seq", "core", "head")
    led = None
    for leader, rim in enumerate(rims):
        pairs = [(i * PEERS + PEERS - 1, (i + 1) * PEERS + leader * MEMBERS) for i in range(RUNS - 1)]
        came = lax.ppermute(rim, everyone, pairs)
        led = came if led is None else led + came
    handed = [led]
    for member in range(1, MEMBERS):
        pairs = [(i, i + member) for i in range(0, RUNS * PEERS, MEMBERS)]
        handed.append(lax.ppermute(led[member], everyone, pairs))
    taps_x = lax.dynamic_slice_in_dim(kernel_x, core * WIDE, WIDE, 1)
    skip = jnp.repeat(lax.dynamic_slice_in_dim(skip_gain, core * MINE, MINE), HEAD_DIM)
    taps = jnp.concatenate([taps_x, kernel_b, kernel_c], 1).astype(F32)
    skip_row = jnp.pad(skip, (0, 2 * STATE))[None]
    taps = jnp.concatenate([taps, skip_row, jnp.zeros((3, WIDE + 2 * STATE), F32)], 0)
    pad = pltpu.VMEM((TILES + 2, TOKENS + 8, 128), F32)
    message, half = call(
        state_kernel,
        (like((RUNS, CUT + 8, 128), BF16), like((PEERS, HALF, 128), BF16)),
        10**9,
        2 * 10**6,
        [pad],
    )(got, taps, *handed)
    slices = lax.all_to_all(message, "seq", split_axis=0, concat_axis=0, tiled=True)
    other = lax.ppermute(half, "core", [(0, 1), (1, 0)])
    vmem = pl.BlockSpec(memory_space=pltpu.VMEM)
    part, c_conv, scale = call(
        local_kernel,
        (
            like((SPANS, SPAN, WIDE), F32),
            like((SPANS, SPAN, STATE), BF16),
            like((SPANS, SPAN, WIDE), F32),
        ),
        10**9,
        8 * 10**6,
        [pad],
        in_specs=[pl.BlockSpec(memory_space=pltpu.SMEM)] + [vmem] * (3 + MEMBERS),
    )(core.astype(jnp.int32).reshape(1), got, other, taps, *handed)
    chained = call(chain_kernel, like((RUNS, CUT, 128), BF16), 10**7, 10**6)(slices)
    state = lax.all_to_all(chained, "seq", split_axis=0, concat_axis=0, tiled=True)
    hbm = pl.BlockSpec(memory_space=pltpu.HBM)
    values = call(
        finish_kernel,
        like((TOKENS, WIDE), BF16),
        10**8,
        3 * 10**6,
        [pltpu.VMEM((TOKENS, WIDE), BF16), pltpu.SemaphoreType.DMA((SPANS,))],
        out_specs=hbm,
    )(part, c_conv, scale, state.reshape(TILES, STATE, 128))
    home = lax.all_to_all(
        values.reshape(PEERS, ROWS, WIDE), ("core", "head"), split_axis=0, concat_axis=0, tiled=True
    )
    width = HEADS * HEAD_DIM
    gate = call(gate_kernel, like((ROWS, width), F32), 10**7, 2 * 10**6)(z_stream)
    return call(
        norm_kernel,
        like((ROWS, width), BF16),
        10**7,
        2 * 10**6,
        [pltpu.VMEM((ROWS, width), BF16), pltpu.SemaphoreType.DMA((GROUPS,))],
        out_specs=hbm,
    )(home, gate, norm_gain.reshape(1, width))


def solution(mesh):
    finer = Mesh(mesh.devices.reshape(RUNS, CORES, RING), ("seq", "core", "head"))
    rows = P(("seq", "core", "head"), None)
    in_specs = (rows,) * 6 + (P(None, "head"),) * 3 + (P("head"), P())
    return jax.shard_map(shards, mesh=finer, in_specs=in_specs, out_specs=rows, check_vma=False)
```

```python
import functools

import jax
import jax.numpy as jnp
from jax import lax
from jax.experimental import pallas as pl
from jax.experimental.pallas import tpu as pltpu
from jax.sharding import Mesh
from jax.sharding import PartitionSpec as P

HEADS = 128
HEAD_DIM = 64
STATE = 128
GROUPS = 8
SPAN = 128
CORES = 2
RING = 8
PEERS = CORES * RING
ROWS = 32
TOKENS = PEERS * ROWS
SPANS = TOKENS // SPAN
FROM = SPAN // ROWS
MINE = HEADS // PEERS
WIDE = MINE * HEAD_DIM
TILES = WIDE // 128
LEADERS = 4
MEMBERS = PEERS // LEADERS
BORDER = 3
RIM = 8 * BORDER
RUNS = 32
HALF = ROWS // CORES
PACK = ROWS * (TILES + 1) + HALF + MINE
CUT = STATE * TILES // RUNS
F32 = jnp.float32
BF16 = jnp.bfloat16
MIB = 1024 * 1024


def call(body, outs, flops, moved, scratch=(), vmem=16, **specs):
    return pl.pallas_call(
        body,
        **specs,
        out_shape=outs,
        scratch_shapes=list(scratch),
        compiler_params=pltpu.CompilerParams(vmem_limit_bytes=vmem * MIB),
        cost_estimate=pl.CostEstimate(flops=flops, bytes_accessed=moved, transcendentals=0),
    )


def like(shape, dtype):
    return jax.ShapeDtypeStruct(shape, dtype)


def silu(x):
    half = 0.5 * x
    return half * jnp.tanh(half) + half


def member_of(leader, member):
    core, side = divmod(leader, 2)
    return core, member if side else RING - 1 - member


def pack_kernel(x_hbm, b_hbm, c_hbm, dt_hbm, decay_hbm, out_ref, *rest):
    rims, (x_ref, b_ref, c_ref, dt_ref, decay_ref, arrived) = rest[:LEADERS], rest[LEADERS:]
    pairs = ((dt_hbm, dt_ref), (decay_hbm, decay_ref), (b_hbm, b_ref), (c_hbm, c_ref), (x_hbm, x_ref))
    copies = [pltpu.make_async_copy(a, b, arrived.at[i]) for i, (a, b) in enumerate(pairs)]
    for copy in copies:
        copy.start()
    copies[0].wait()
    copies[1].wait()
    steps = jnp.transpose(dt_ref[...].astype(F32))
    decays = jnp.transpose(decay_ref[...].astype(F32))
    at = TILES * ROWS
    for copy in copies[2:4]:
        copy.wait()
    for core in range(CORES):
        for ring in range(RING):
            peer = core * RING + ring
            out_ref[peer, at : at + ROWS, :] = b_ref[:, ring * 128 : (ring + 1) * 128]
            rows = slice(core * HALF, (core + 1) * HALF)
            out_ref[peer, at + ROWS : at + ROWS + HALF, :] = c_ref[rows, ring * 128 : (ring + 1) * 128]
            head = (ring * CORES + core) * MINE
            rest = jnp.zeros((MINE, 128 - 2 * ROWS), F32)
            both = jnp.concatenate([steps[head : head + MINE], decays[head : head + MINE], rest], 1)
            out_ref[peer, at + ROWS + HALF :, :] = both.astype(BF16)
    copies[4].wait()
    for core in range(CORES):
        for ring in range(RING):
            for tile in range(TILES):
                column = ring * CORES * WIDE + core * WIDE + tile * 128
                out_ref[core * RING + ring, tile * ROWS : (tile + 1) * ROWS, :] = x_ref[:, column : column + 128]
    rows = slice(ROWS - 16, ROWS)
    for leader in range(LEADERS):
        for member in range(MEMBERS):
            core, ring = member_of(leader, member)
            column = (ring * CORES + core) * WIDE
            pieces = [x_ref[rows, column + tile * 128 : column + (tile + 1) * 128] for tile in range(TILES)]
            pieces += [ref[rows, ring * 128 : (ring + 1) * 128] for ref in (b_ref, c_ref)]
            pieces = [piece.astype(F32) for piece in pieces]
            whole = [piece[16 - BORDER + token :][:1] for token in range(BORDER) for piece in pieces + pieces[:2]]
            rims[leader][member] = jnp.concatenate(whole, 0).astype(BF16)


def raw(r_ref, span, tile):
    return r_ref[span * FROM : (span + 1) * FROM, tile * ROWS : (tile + 1) * ROWS, :].reshape(SPAN, 128)


def c_rows(r_ref):
    at = (TILES + 1) * ROWS
    return r_ref[:, at : at + HALF, :]


def fill(r_ref, rims, pad_ref, tiles):
    rim = rims[0][0].astype(F32)
    for ref in rims[1:]:
        rim = rim + ref[...].astype(F32)
    for tile in tiles:
        tokens = [rim[token * 8 + tile : token * 8 + tile + 1] for token in range(BORDER)]
        edge = jnp.concatenate([jnp.zeros((8 - BORDER, 128), F32)] + tokens, 0)
        pad_ref[tile, 0:8, :] = edge
        if tile > TILES:
            continue
        for span in range(SPANS):
            pad_ref[tile, 8 + span * SPAN : 8 + (span + 1) * SPAN, :] = raw(r_ref, span, tile).astype(F32)


def conv_silu(taps_ref, pad_ref, span, tile):
    lanes = slice(tile * 128, (tile + 1) * 128)
    at = span * SPAN
    whole = pad_ref[tile, at : at + SPAN + 8, :]
    total = whole[8:] * taps_ref[3:4, lanes]
    for tap in range(3):
        total = total + pltpu.roll(whole, 3 - tap, 0)[8:] * taps_ref[tap : tap + 1, lanes]
    return silu(total).astype(BF16)


def rows_of(r_ref):
    at = (TILES + 1) * ROWS + HALF
    steps, decays = [], []
    for span in range(SPANS):
        parts = [r_ref[span * FROM + m, at : at + MINE, :].astype(F32) for m in range(FROM)]
        steps.append(jnp.concatenate([part[:, :ROWS] for part in parts], 1))
        decays.append(jnp.concatenate([part[:, ROWS : 2 * ROWS] for part in parts], 1))
    decays = jnp.concatenate(decays, 0)
    row = lax.broadcasted_iota(jnp.int32, (SPAN, SPAN), 0)
    column = lax.broadcasted_iota(jnp.int32, (SPAN, SPAN), 1)
    upper = (row <= column).astype(F32).astype(BF16)
    running = jnp.dot(decays.astype(BF16), upper, preferred_element_type=F32)
    return jnp.concatenate(steps, 0), running


def terms(x, count):
    parts = []
    for _ in range(count):
        parts.append(x.astype(BF16))
        x = x - parts[-1].astype(F32)
    return parts


def own_lanes(count):
    row = lax.broadcasted_iota(jnp.int32, (count * MINE, WIDE), 0)
    column = lax.broadcasted_iota(jnp.int32, (count * MINE, WIDE), 1)
    return (lax.rem(row, MINE) == lax.div(column, HEAD_DIM)).astype(F32).astype(BF16)


def widen(per_head, lanes, count):
    stack = jnp.concatenate([part.astype(F32) for part in terms(per_head, count)], 0).astype(BF16)
    return lax.dot_general(stack, lanes, (((0,), (0,)), ((), ())), preferred_element_type=F32)


def span_state(taps_ref, pad_ref, span, tail):
    b_conv = conv_silu(taps_ref, pad_ref, span, TILES)
    parts = [conv_silu(taps_ref, pad_ref, span, tile) for tile in range(TILES)]
    x_conv = jnp.concatenate(parts, 1)
    weighted = (x_conv.astype(F32) * tail).astype(BF16)
    b_turned = jnp.transpose(b_conv.astype(F32)).astype(BF16)
    return x_conv, b_conv, jnp.dot(b_turned, weighted, preferred_element_type=F32)


def of_span(x, span):
    return x[span * MINE : (span + 1) * MINE]


def state_kernel(r_ref, taps_ref, *rest):
    rims, (message_ref, half_ref, pad_ref) = rest[:MEMBERS], rest[MEMBERS:]
    half_ref[...] = c_rows(r_ref)
    fill(r_ref, rims, pad_ref, range(TILES + 1))
    steps, running = rows_of(r_ref)
    lanes = own_lanes(2)
    tails = jnp.exp(running[:, SPAN - 1 :] - running) * steps
    last = [of_span(running, span)[:, SPAN - 1 :] for span in range(SPANS)]
    factors = jnp.exp(jnp.concatenate(last + [last[0] + last[1] + last[2] + last[3]], 1))
    factors = jnp.concatenate([factors, jnp.zeros((MINE, SPAN - SPANS - 1), F32)], 1)
    factors = widen(factors, lanes, 2)
    state = None
    for span in range(SPANS):
        _, _, fresh = span_state(taps_ref, pad_ref, span, widen(of_span(tails, span), lanes, 2))
        state = fresh if span == 0 else state * factors[span : span + 1] + fresh
    scale = factors[SPANS : SPANS + 1]
    coarse = scale.astype(BF16).astype(F32)
    tail = jnp.concatenate([coarse, scale - coarse, jnp.zeros((6, WIDE), F32)], 0)
    for tile in range(TILES):
        here = slice(tile * 128, (tile + 1) * 128)
        for cut in range(STATE // CUT):
            whole = jnp.concatenate([state[cut * CUT : (cut + 1) * CUT, here], tail[:, here]], 0)
            message_ref[tile * (STATE // CUT) + cut] = whole.astype(BF16)


def local_kernel(core_ref, r_ref, other_ref, taps_ref, *rest):
    rims, (part_ref, c_ref, scale_ref, pad_ref) = rest[:MEMBERS], rest[MEMBERS:]
    fill(r_ref, rims, pad_ref, range(TILES + 2))
    first = core_ref[0] == 0
    own, other = c_rows(r_ref).astype(F32), other_ref[...].astype(F32)
    whole = jnp.concatenate([jnp.where(first, own, other), jnp.where(first, other, own)], 1)
    pad_ref[TILES + 1, 8:, :] = whole.reshape(TOKENS, 128)
    row = lax.broadcasted_iota(jnp.int32, (SPAN, SPAN), 0)
    column = lax.broadcasted_iota(jnp.int32, (SPAN, SPAN), 1)
    causal = row >= column
    low = lax.broadcasted_iota(jnp.int32, (SPAN, 128), 1) < HEAD_DIM
    steps, running = rows_of(r_ref)
    lanes_two, lanes_three = own_lanes(2), own_lanes(3)
    tails = jnp.exp(running[:, SPAN - 1 :] - running) * steps
    turned = jnp.transpose(jnp.concatenate([running, jnp.zeros((SPAN - SPANS * MINE, SPAN), F32)], 0))
    before = jnp.zeros((MINE, 1), F32)
    state = None
    for span in range(SPANS):
        c_conv = conv_silu(taps_ref, pad_ref, span, TILES + 1)
        c_ref[span] = c_conv
        x_conv, b_conv, fresh = span_state(taps_ref, pad_ref, span, widen(of_span(tails, span), lanes_two, 2))
        scores = lax.dot_general(c_conv, b_conv, (((1,), (1,)), ((), ())), preferred_element_type=F32)
        here = of_span(running, span)
        grown = widen(jnp.exp(here), lanes_two, 2)
        scale_ref[span] = grown if span == 0 else widen(jnp.exp(here + before), lanes_two, 2)
        outs = []
        for tile in range(TILES):
            lanes = slice(tile * 128, (tile + 1) * 128)
            pair = []
            for head in (2 * tile, 2 * tile + 1):
                at = span * MINE + head
                gap = turned[:, at : at + 1] - running[at : at + 1]
                decay = jnp.exp(jnp.where(causal, gap, -1e30)) * steps[at : at + 1]
                pair.append((decay * scores).astype(BF16))
            both = jnp.dot(jnp.concatenate(pair, 0), x_conv[:, lanes], preferred_element_type=F32)
            outs.append(jnp.where(low, both[:SPAN], both[SPAN:]))
        out = jnp.concatenate(outs, 1) + x_conv.astype(F32) * taps_ref[4:5, :WIDE]
        if span:
            out = out + jnp.dot(c_conv, state.astype(BF16), preferred_element_type=F32) * grown
        part_ref[span] = out
        before = before + here[:, SPAN - 1 :]
        if span == 0:
            state = fresh
        elif span < SPANS - 1:
            state = state * grown[SPAN - 1 :] + fresh


def chain_kernel(all_ref, out_ref):
    state = jnp.zeros((CUT, 128), F32)
    for run in range(RUNS):
        out_ref[run] = state.astype(BF16)
        if run < RUNS - 1:
            here = all_ref[run].astype(F32)
            state = state * (here[CUT : CUT + 1] + here[CUT + 1 : CUT + 2]) + here[:CUT]


def finish_kernel(part_ref, c_ref, scale_ref, state_ref, out_hbm, out_ref, sent):
    state = jnp.concatenate([state_ref[tile] for tile in range(TILES)], 1)
    copies = []
    for span in range(SPANS):
        rows = slice(span * SPAN, (span + 1) * SPAN)
        inter = jnp.dot(c_ref[span], state, preferred_element_type=F32)
        out_ref[rows, :] = (part_ref[span] + inter * scale_ref[span]).astype(BF16)
        copies.append(pltpu.make_async_copy(out_ref.at[rows, :], out_hbm.at[rows, :], sent.at[span]))
        copies[-1].start()
    for copy in copies:
        copy.wait()


def gate_kernel(z_ref, out_ref):
    out_ref[...] = silu(z_ref[...].astype(F32))


def norm_kernel(values_ref, gate_ref, gain_ref, out_hbm, out_ref, sent):
    copies = []
    for group in range(GROUPS):
        whole = slice(group * CORES * WIDE, (group + 1) * CORES * WIDE)
        here = jnp.concatenate([values_ref[core * RING + group] for core in range(CORES)], 1)
        here = here.astype(F32) * gate_ref[:, whole]
        square = jnp.sum(here * here, axis=1, keepdims=True)
        scale = lax.rsqrt(square * (1.0 / (CORES * WIDE)) + 1e-05)
        out_ref[:, whole] = (here * scale * gain_ref[:, whole].astype(F32)).astype(BF16)
        copies.append(pltpu.make_async_copy(out_ref.at[:, whole], out_hbm.at[:, whole], sent.at[group]))
        copies[-1].start()
    for copy in copies:
        copy.wait()


def shards(
    x_stream,
    z_stream,
    b_stream,
    c_stream,
    dt_stream,
    decay_stream,
    kernel_x,
    kernel_b,
    kernel_c,
    skip_gain,
    norm_gain,
):
    core = lax.axis_index("core")
    streams = (x_stream, b_stream, c_stream, dt_stream, decay_stream)
    packed, *rims = call(
        pack_kernel,
        (like((PEERS, PACK, 128), BF16),) + (like((MEMBERS, RIM, 128), BF16),) * LEADERS,
        0,
        2 * PEERS * PACK * 256,
        [pltpu.VMEM(stream.shape, BF16) for stream in streams] + [pltpu.SemaphoreType.DMA((5,))],
        vmem=60,
        in_specs=[pl.BlockSpec(memory_space=pltpu.HBM)] * 5,
    )(*streams)
    got = lax.all_to_all(packed, ("core", "head"), split_axis=0, concat_axis=0, tiled=True)
    everyone = ("seq", "core", "head")
    led = None
    place = [[core * RING + ring for core, ring in (member_of(i, j) for j in range(MEMBERS))] for i in range(LEADERS)]
    for leader, rim in enumerate(rims):
        pairs = [(i * PEERS + PEERS - 1, (i + 1) * PEERS + place[leader][0]) for i in range(RUNS - 1)]
        came = lax.ppermute(rim, everyone, pairs)
        led = came if led is None else led + came
    handed = [led]
    for member in range(1, MEMBERS):
        pairs = [(i * PEERS + devices[0], i * PEERS + devices[member]) for i in range(RUNS) for devices in place]
        handed.append(lax.ppermute(led[member], everyone, pairs))
    taps_x = lax.dynamic_slice_in_dim(kernel_x, core * WIDE, WIDE, 1)
    skip = jnp.repeat(lax.dynamic_slice_in_dim(skip_gain, core * MINE, MINE), HEAD_DIM)
    taps = jnp.concatenate([taps_x, kernel_b, kernel_c], 1).astype(F32)
    skip_row = jnp.pad(skip, (0, 2 * STATE))[None]
    taps = jnp.concatenate([taps, skip_row, jnp.zeros((3, WIDE + 2 * STATE), F32)], 0)
    pad = pltpu.VMEM((TILES + 2, TOKENS + 8, 128), F32)
    message, half = call(
        state_kernel,
        (like((RUNS, CUT + 8, 128), BF16), like((PEERS, HALF, 128), BF16)),
        10**9,
        2 * 10**6,
        [pad],
    )(got, taps, *handed)
    slices = lax.all_to_all(message, "seq", split_axis=0, concat_axis=0, tiled=True)
    other = lax.ppermute(half, "core", [(0, 1), (1, 0)])
    vmem = pl.BlockSpec(memory_space=pltpu.VMEM)
    part, c_conv, scale = call(
        local_kernel,
        (
            like((SPANS, SPAN, WIDE), F32),
            like((SPANS, SPAN, STATE), BF16),
            like((SPANS, SPAN, WIDE), F32),
        ),
        10**9,
        8 * 10**6,
        [pad],
        in_specs=[pl.BlockSpec(memory_space=pltpu.SMEM)] + [vmem] * (3 + MEMBERS),
    )(core.astype(jnp.int32).reshape(1), got, other, taps, *handed)
    chained = call(chain_kernel, like((RUNS, CUT, 128), BF16), 10**7, 10**6)(slices)
    state = lax.all_to_all(chained, "seq", split_axis=0, concat_axis=0, tiled=True)
    hbm = pl.BlockSpec(memory_space=pltpu.HBM)
    values = call(
        finish_kernel,
        like((TOKENS, WIDE), BF16),
        10**8,
        3 * 10**6,
        [pltpu.VMEM((TOKENS, WIDE), BF16), pltpu.SemaphoreType.DMA((SPANS,))],
        out_specs=hbm,
    )(part, c_conv, scale, state.reshape(TILES, STATE, 128))
    home = lax.all_to_all(
        values.reshape(PEERS, ROWS, WIDE), ("core", "head"), split_axis=0, concat_axis=0, tiled=True
    )
    width = HEADS * HEAD_DIM
    gate = call(gate_kernel, like((ROWS, width), F32), 10**7, 2 * 10**6)(z_stream)
    return call(
        norm_kernel,
        like((ROWS, width), BF16),
        10**7,
        2 * 10**6,
        [pltpu.VMEM((ROWS, width), BF16), pltpu.SemaphoreType.DMA((GROUPS,))],
        out_specs=hbm,
    )(home, gate, norm_gain.reshape(1, width))


def solution(mesh):
    finer = Mesh(mesh.devices.reshape(RUNS, CORES, RING), ("seq", "core", "head"))
    rows = P(("seq", "core", "head"), None)
    in_specs = (rows,) * 6 + (P(None, "head"),) * 3 + (P("head"), P())
    return jax.shard_map(shards, mesh=finer, in_specs=in_specs, out_specs=rows, check_vma=False)
```

```python
import functools

import jax
import jax.numpy as jnp
from jax import lax
from jax.experimental import pallas as pl
from jax.experimental.pallas import tpu as pltpu
from jax.sharding import Mesh
from jax.sharding import PartitionSpec as P

HEADS = 128
HEAD_DIM = 64
STATE = 128
GROUPS = 8
SPAN = 128
CORES = 2
RING = 8
PEERS = CORES * RING
ROWS = 32
TOKENS = PEERS * ROWS
SPANS = TOKENS // SPAN
FROM = SPAN // ROWS
MINE = HEADS // PEERS
WIDE = MINE * HEAD_DIM
TILES = WIDE // 128
LEADERS = 4
MEMBERS = PEERS // LEADERS
BORDER = 3
RIM = 8 * BORDER
RUNS = 32
HALF = ROWS // CORES
PACK = ROWS * (TILES + 1) + HALF + MINE
CUT = STATE * TILES // RUNS
F32 = jnp.float32
BF16 = jnp.bfloat16
MIB = 1024 * 1024


def call(body, outs, flops, moved, scratch=(), vmem=16, **specs):
    return pl.pallas_call(
        body,
        **specs,
        out_shape=outs,
        scratch_shapes=list(scratch),
        compiler_params=pltpu.CompilerParams(vmem_limit_bytes=vmem * MIB),
        cost_estimate=pl.CostEstimate(flops=flops, bytes_accessed=moved, transcendentals=0),
    )


def like(shape, dtype):
    return jax.ShapeDtypeStruct(shape, dtype)


def silu(x):
    half = 0.5 * x
    return half * jnp.tanh(half) + half


def member_of(leader, member):
    core, side = divmod(leader, 2)
    return core, member if side else RING - 1 - member


def pack_kernel(x_hbm, b_hbm, c_hbm, dt_hbm, decay_hbm, out_ref, *rest):
    rims, (x_ref, b_ref, c_ref, dt_ref, decay_ref, arrived) = rest[:LEADERS], rest[LEADERS:]
    pairs = ((dt_hbm, dt_ref), (decay_hbm, decay_ref), (b_hbm, b_ref), (c_hbm, c_ref), (x_hbm, x_ref))
    copies = [pltpu.make_async_copy(a, b, arrived.at[i]) for i, (a, b) in enumerate(pairs)]
    for copy in copies:
        copy.start()
    copies[0].wait()
    copies[1].wait()
    steps = jnp.transpose(dt_ref[...].astype(F32))
    decays = jnp.transpose(decay_ref[...].astype(F32))
    at = TILES * ROWS
    for copy in copies[2:4]:
        copy.wait()
    for core in range(CORES):
        for ring in range(RING):
            peer = core * RING + ring
            out_ref[peer, at : at + ROWS, :] = b_ref[:, ring * 128 : (ring + 1) * 128]
            rows = slice(core * HALF, (core + 1) * HALF)
            out_ref[peer, at + ROWS : at + ROWS + HALF, :] = c_ref[rows, ring * 128 : (ring + 1) * 128]
            head = (ring * CORES + core) * MINE
            rest = jnp.zeros((MINE, 128 - 2 * ROWS), F32)
            both = jnp.concatenate([steps[head : head + MINE], decays[head : head + MINE], rest], 1)
            out_ref[peer, at + ROWS + HALF :, :] = both.astype(BF16)
    copies[4].wait()
    for core in range(CORES):
        for ring in range(RING):
            for tile in range(TILES):
                column = ring * CORES * WIDE + core * WIDE + tile * 128
                out_ref[core * RING + ring, tile * ROWS : (tile + 1) * ROWS, :] = x_ref[:, column : column + 128]
    rows = slice(ROWS - 16, ROWS)
    for leader in range(LEADERS):
        for member in range(MEMBERS):
            core, ring = member_of(leader, member)
            column = (ring * CORES + core) * WIDE
            pieces = [x_ref[rows, column + tile * 128 : column + (tile + 1) * 128] for tile in range(TILES)]
            pieces += [ref[rows, ring * 128 : (ring + 1) * 128] for ref in (b_ref, c_ref)]
            pieces = [piece.astype(F32) for piece in pieces]
            whole = [piece[16 - BORDER + token :][:1] for token in range(BORDER) for piece in pieces + pieces[:2]]
            rims[leader][member] = jnp.concatenate(whole, 0).astype(BF16)


def raw(r_ref, span, tile):
    return r_ref[span * FROM : (span + 1) * FROM, tile * ROWS : (tile + 1) * ROWS, :].reshape(SPAN, 128)


def c_rows(r_ref):
    at = (TILES + 1) * ROWS
    return r_ref[:, at : at + HALF, :]


def fill(r_ref, rims, pad_ref, tiles):
    rim = rims[0][0].astype(F32)
    for ref in rims[1:]:
        rim = rim + ref[...].astype(F32)
    for tile in tiles:
        tokens = [rim[token * 8 + tile : token * 8 + tile + 1] for token in range(BORDER)]
        edge = jnp.concatenate([jnp.zeros((8 - BORDER, 128), F32)] + tokens, 0)
        pad_ref[tile, 0:8, :] = edge
        if tile > TILES:
            continue
        for span in range(SPANS):
            pad_ref[tile, 8 + span * SPAN : 8 + (span + 1) * SPAN, :] = raw(r_ref, span, tile).astype(F32)


def conv_silu(taps_ref, pad_ref, span, tile):
    lanes = slice(tile * 128, (tile + 1) * 128)
    at = 8 - BORDER + span * SPAN
    total = pad_ref[tile, at : at + SPAN, :] * taps_ref[0:1, lanes]
    for tap in range(1, BORDER + 1):
        total = total + pad_ref[tile, at + tap : at + tap + SPAN, :] * taps_ref[tap : tap + 1, lanes]
    return silu(total).astype(BF16)


def rows_of(r_ref):
    at = (TILES + 1) * ROWS + HALF
    steps, decays = [], []
    for span in range(SPANS):
        parts = [r_ref[span * FROM + m, at : at + MINE, :].astype(F32) for m in range(FROM)]
        steps.append(jnp.concatenate([part[:, :ROWS] for part in parts], 1))
        decays.append(jnp.concatenate([part[:, ROWS : 2 * ROWS] for part in parts], 1))
    decays = jnp.concatenate(decays, 0)
    row = lax.broadcasted_iota(jnp.int32, (SPAN, SPAN), 0)
    column = lax.broadcasted_iota(jnp.int32, (SPAN, SPAN), 1)
    upper = (row <= column).astype(F32).astype(BF16)
    running = jnp.dot(decays.astype(BF16), upper, preferred_element_type=F32)
    return jnp.concatenate(steps, 0), running


def terms(x, count):
    parts = []
    for _ in range(count):
        parts.append(x.astype(BF16))
        x = x - parts[-1].astype(F32)
    return parts


def own_lanes(count):
    row = lax.broadcasted_iota(jnp.int32, (count * MINE, WIDE), 0)
    column = lax.broadcasted_iota(jnp.int32, (count * MINE, WIDE), 1)
    return (lax.rem(row, MINE) == lax.div(column, HEAD_DIM)).astype(F32).astype(BF16)


def widen(per_head, lanes, count):
    stack = jnp.concatenate([part.astype(F32) for part in terms(per_head, count)], 0).astype(BF16)
    return lax.dot_general(stack, lanes, (((0,), (0,)), ((), ())), preferred_element_type=F32)


def span_state(taps_ref, pad_ref, span, tail):
    b_conv = conv_silu(taps_ref, pad_ref, span, TILES)
    parts = [conv_silu(taps_ref, pad_ref, span, tile) for tile in range(TILES)]
    x_conv = jnp.concatenate(parts, 1)
    weighted = (x_conv.astype(F32) * tail).astype(BF16)
    b_turned = jnp.transpose(b_conv.astype(F32)).astype(BF16)
    return x_conv, b_conv, jnp.dot(b_turned, weighted, preferred_element_type=F32)


def of_span(x, span):
    return x[span * MINE : (span + 1) * MINE]


def state_kernel(r_ref, taps_ref, *rest):
    rims, (message_ref, half_ref, pad_ref) = rest[:MEMBERS], rest[MEMBERS:]
    half_ref[...] = c_rows(r_ref)
    fill(r_ref, rims, pad_ref, range(TILES + 1))
    steps, running = rows_of(r_ref)
    lanes = own_lanes(2)
    tails = jnp.exp(running[:, SPAN - 1 :] - running) * steps
    last = [of_span(running, span)[:, SPAN - 1 :] for span in range(SPANS)]
    factors = jnp.exp(jnp.concatenate(last + [last[0] + last[1] + last[2] + last[3]], 1))
    factors = jnp.concatenate([factors, jnp.zeros((MINE, SPAN - SPANS - 1), F32)], 1)
    factors = widen(factors, lanes, 2)
    state = None
    for span in range(SPANS):
        _, _, fresh = span_state(taps_ref, pad_ref, span, widen(of_span(tails, span), lanes, 2))
        state = fresh if span == 0 else state * factors[span : span + 1] + fresh
    scale = factors[SPANS : SPANS + 1]
    coarse = scale.astype(BF16).astype(F32)
    tail = jnp.concatenate([coarse, scale - coarse, jnp.zeros((6, WIDE), F32)], 0)
    for tile in range(TILES):
        here = slice(tile * 128, (tile + 1) * 128)
        for cut in range(STATE // CUT):
            whole = jnp.concatenate([state[cut * CUT : (cut + 1) * CUT, here], tail[:, here]], 0)
            message_ref[tile * (STATE // CUT) + cut] = whole.astype(BF16)


def local_kernel(core_ref, r_ref, other_ref, taps_ref, *rest):
    rims, (part_ref, c_ref, scale_ref, pad_ref) = rest[:MEMBERS], rest[MEMBERS:]
    fill(r_ref, rims, pad_ref, range(TILES + 2))
    first = core_ref[0] == 0
    own, other = c_rows(r_ref).astype(F32), other_ref[...].astype(F32)
    whole = jnp.concatenate([jnp.where(first, own, other), jnp.where(first, other, own)], 1)
    pad_ref[TILES + 1, 8:, :] = whole.reshape(TOKENS, 128)
    row = lax.broadcasted_iota(jnp.int32, (SPAN, SPAN), 0)
    column = lax.broadcasted_iota(jnp.int32, (SPAN, SPAN), 1)
    causal = row >= column
    low = lax.broadcasted_iota(jnp.int32, (SPAN, 128), 1) < HEAD_DIM
    steps, running = rows_of(r_ref)
    lanes_two, lanes_three = own_lanes(2), own_lanes(3)
    tails = jnp.exp(running[:, SPAN - 1 :] - running) * steps
    turned = jnp.transpose(jnp.concatenate([running, jnp.zeros((SPAN - SPANS * MINE, SPAN), F32)], 0))
    before = jnp.zeros((MINE, 1), F32)
    state = None
    for span in range(SPANS):
        c_conv = conv_silu(taps_ref, pad_ref, span, TILES + 1)
        c_ref[span] = c_conv
        x_conv, b_conv, fresh = span_state(taps_ref, pad_ref, span, widen(of_span(tails, span), lanes_two, 2))
        scores = lax.dot_general(c_conv, b_conv, (((1,), (1,)), ((), ())), preferred_element_type=F32)
        here = of_span(running, span)
        grown = widen(jnp.exp(here), lanes_two, 2)
        scale_ref[span] = grown if span == 0 else widen(jnp.exp(here + before), lanes_two, 2)
        outs = []
        for tile in range(TILES):
            lanes = slice(tile * 128, (tile + 1) * 128)
            pair = []
            for head in (2 * tile, 2 * tile + 1):
                at = span * MINE + head
                gap = turned[:, at : at + 1] - running[at : at + 1]
                decay = jnp.exp(jnp.where(causal, gap, -1e30)) * steps[at : at + 1]
                pair.append((decay * scores).astype(BF16))
            both = jnp.dot(jnp.concatenate(pair, 0), x_conv[:, lanes], preferred_element_type=F32)
            outs.append(jnp.where(low, both[:SPAN], both[SPAN:]))
        out = jnp.concatenate(outs, 1) + x_conv.astype(F32) * taps_ref[4:5, :WIDE]
        if span:
            out = out + jnp.dot(c_conv, state.astype(BF16), preferred_element_type=F32) * grown
        part_ref[span] = out
        before = before + here[:, SPAN - 1 :]
        if span == 0:
            state = fresh
        elif span < SPANS - 1:
            state = state * grown[SPAN - 1 :] + fresh


def chain_kernel(all_ref, out_ref):
    state = jnp.zeros((CUT, 128), F32)
    for run in range(RUNS):
        out_ref[run] = state.astype(BF16)
        if run < RUNS - 1:
            here = all_ref[run].astype(F32)
            state = state * (here[CUT : CUT + 1] + here[CUT + 1 : CUT + 2]) + here[:CUT]


def finish_kernel(part_ref, c_ref, scale_ref, state_ref, out_ref):
    state = jnp.concatenate([state_ref[tile] for tile in range(TILES)], 1)
    for span in range(SPANS):
        inter = jnp.dot(c_ref[span], state, preferred_element_type=F32)
        out_ref[span * SPAN : (span + 1) * SPAN, :] = (part_ref[span] + inter * scale_ref[span]).astype(BF16)


def gate_kernel(z_ref, gain_ref, gate_ref, row_ref):
    gate_ref[...] = silu(z_ref[...].astype(F32))
    row_ref[...] = gain_ref[...].astype(F32)


def norm_kernel(values_ref, gate_ref, gain_ref, out_hbm, out_ref, sent):
    copies = []
    for group in range(GROUPS):
        whole = slice(group * CORES * WIDE, (group + 1) * CORES * WIDE)
        here = jnp.concatenate([values_ref[core * RING + group] for core in range(CORES)], 1)
        here = here.astype(F32) * gate_ref[:, whole]
        square = jnp.sum(here * here, axis=1, keepdims=True)
        scale = lax.rsqrt(square * (1.0 / (CORES * WIDE)) + 1e-05)
        out_ref[:, whole] = (here * scale * gain_ref[:, whole]).astype(BF16)
        copies.append(pltpu.make_async_copy(out_ref.at[:, whole], out_hbm.at[:, whole], sent.at[group]))
        copies[-1].start()
    for copy in copies:
        copy.wait()


def shards(
    x_stream,
    z_stream,
    b_stream,
    c_stream,
    dt_stream,
    decay_stream,
    kernel_x,
    kernel_b,
    kernel_c,
    skip_gain,
    norm_gain,
):
    core = lax.axis_index("core")
    streams = (x_stream, b_stream, c_stream, dt_stream, decay_stream)
    packed, *rims = call(
        pack_kernel,
        (like((PEERS, PACK, 128), BF16),) + (like((MEMBERS, RIM, 128), BF16),) * LEADERS,
        0,
        2 * PEERS * PACK * 256,
        [pltpu.VMEM(stream.shape, BF16) for stream in streams] + [pltpu.SemaphoreType.DMA((5,))],
        vmem=60,
        in_specs=[pl.BlockSpec(memory_space=pltpu.HBM)] * 5,
    )(*streams)
    got = lax.all_to_all(packed, ("core", "head"), split_axis=0, concat_axis=0, tiled=True)
    everyone = ("seq", "core", "head")
    led = None
    place = [[core * RING + ring for core, ring in (member_of(i, j) for j in range(MEMBERS))] for i in range(LEADERS)]
    for leader, rim in enumerate(rims):
        pairs = [(i * PEERS + PEERS - 1, (i + 1) * PEERS + place[leader][0]) for i in range(RUNS - 1)]
        came = lax.ppermute(rim, everyone, pairs)
        led = came if led is None else led + came
    handed = [led]
    for member in range(1, MEMBERS):
        pairs = [(i * PEERS + devices[0], i * PEERS + devices[member]) for i in range(RUNS) for devices in place]
        handed.append(lax.ppermute(led[member], everyone, pairs))
    taps_x = lax.dynamic_slice_in_dim(kernel_x, core * WIDE, WIDE, 1)
    skip = jnp.repeat(lax.dynamic_slice_in_dim(skip_gain, core * MINE, MINE), HEAD_DIM)
    taps = jnp.concatenate([taps_x, kernel_b, kernel_c], 1).astype(F32)
    skip_row = jnp.pad(skip, (0, 2 * STATE))[None]
    taps = jnp.concatenate([taps, skip_row, jnp.zeros((3, WIDE + 2 * STATE), F32)], 0)
    pad = pltpu.VMEM((TILES + 2, TOKENS + 8, 128), F32)
    width = HEADS * HEAD_DIM
    taps, gain_held = lax.optimization_barrier((taps, norm_gain.reshape(1, width)))
    message, half = call(
        state_kernel,
        (like((RUNS, CUT + 8, 128), BF16), like((PEERS, HALF, 128), BF16)),
        10**9,
        2 * 10**6,
        [pad],
    )(got, taps, *handed)
    slices = lax.all_to_all(message, "seq", split_axis=0, concat_axis=0, tiled=True)
    other = lax.ppermute(half, "core", [(0, 1), (1, 0)])
    vmem = pl.BlockSpec(memory_space=pltpu.VMEM)
    part, c_conv, scale = call(
        local_kernel,
        (
            like((SPANS, SPAN, WIDE), F32),
            like((SPANS, SPAN, STATE), BF16),
            like((SPANS, SPAN, WIDE), F32),
        ),
        10**9,
        8 * 10**6,
        [pad],
        in_specs=[pl.BlockSpec(memory_space=pltpu.SMEM)] + [vmem] * (3 + MEMBERS),
    )(core.astype(jnp.int32).reshape(1), got, other, taps, *handed)
    z_held, slices = lax.optimization_barrier((z_stream, slices))
    gate, gain = call(
        gate_kernel, (like((ROWS, width), F32), like((1, width), F32)), 10**7, 2 * 10**6
    )(z_held, gain_held)
    part, gate, gain = lax.optimization_barrier((part, gate, gain))
    chained = call(chain_kernel, like((RUNS, CUT, 128), BF16), 10**7, 10**6)(slices)
    state = lax.all_to_all(chained, "seq", split_axis=0, concat_axis=0, tiled=True)
    hbm = pl.BlockSpec(memory_space=pltpu.HBM)
    values = call(
        finish_kernel,
        like((TOKENS, WIDE), BF16),
        10**8,
        3 * 10**6,
    )(part, c_conv, scale, state.reshape(TILES, STATE, 128))
    home = lax.all_to_all(
        values.reshape(PEERS, ROWS, WIDE), ("core", "head"), split_axis=0, concat_axis=0, tiled=True
    )
    return call(
        norm_kernel,
        like((ROWS, width), BF16),
        10**7,
        2 * 10**6,
        [pltpu.VMEM((ROWS, width), BF16), pltpu.SemaphoreType.DMA((GROUPS,))],
        out_specs=hbm,
    )(home, gate, gain)


def solution(mesh):
    finer = Mesh(mesh.devices.reshape(RUNS, CORES, RING), ("seq", "core", "head"))
    rows = P(("seq", "core", "head"), None)
    in_specs = (rows,) * 6 + (P(None, "head"),) * 3 + (P("head"), P())
    return jax.shard_map(shards, mesh=finer, in_specs=in_specs, out_specs=rows, check_vma=False)
```

```python
import functools

import jax
import jax.numpy as jnp
from jax import lax
from jax.experimental import pallas as pl
from jax.experimental.pallas import tpu as pltpu
from jax.sharding import Mesh
from jax.sharding import PartitionSpec as P

HEADS = 128
HEAD_DIM = 64
STATE = 128
GROUPS = 8
SPAN = 128
CORES = 2
RING = 8
PEERS = CORES * RING
ROWS = 32
TOKENS = PEERS * ROWS
SPANS = TOKENS // SPAN
FROM = SPAN // ROWS
MINE = HEADS // PEERS
WIDE = MINE * HEAD_DIM
TILES = WIDE // 128
LEADERS = 4
MEMBERS = PEERS // LEADERS
BORDER = 3
RIM = 8 * BORDER
RUNS = 32
HALF = ROWS // CORES
PACK = ROWS * (TILES + 1) + HALF + MINE
CUT = STATE * TILES // RUNS
F32 = jnp.float32
BF16 = jnp.bfloat16
MIB = 1024 * 1024


def call(body, outs, flops, moved, scratch=(), vmem=16, **specs):
    return pl.pallas_call(
        body,
        **specs,
        out_shape=outs,
        scratch_shapes=list(scratch),
        compiler_params=pltpu.CompilerParams(vmem_limit_bytes=vmem * MIB),
        cost_estimate=pl.CostEstimate(flops=flops, bytes_accessed=moved, transcendentals=0),
    )


def like(shape, dtype):
    return jax.ShapeDtypeStruct(shape, dtype)


def silu(x):
    half = 0.5 * x
    return half * jnp.tanh(half) + half


def member_of(leader, member):
    core, side = divmod(leader, 2)
    return core, member if side else RING - 1 - member


def pack_kernel(x_hbm, b_hbm, c_hbm, dt_hbm, decay_hbm, out_ref, *rest):
    rims, (x_ref, b_ref, c_ref, dt_ref, decay_ref, arrived) = rest[:LEADERS], rest[LEADERS:]
    pairs = ((dt_hbm, dt_ref), (decay_hbm, decay_ref), (b_hbm, b_ref), (c_hbm, c_ref), (x_hbm, x_ref))
    copies = [pltpu.make_async_copy(a, b, arrived.at[i]) for i, (a, b) in enumerate(pairs)]
    for copy in copies:
        copy.start()
    copies[0].wait()
    copies[1].wait()
    steps = jnp.transpose(dt_ref[...].astype(F32))
    decays = jnp.transpose(decay_ref[...].astype(F32))
    at = TILES * ROWS
    for copy in copies[2:4]:
        copy.wait()
    for core in range(CORES):
        for ring in range(RING):
            peer = core * RING + ring
            out_ref[peer, at : at + ROWS, :] = b_ref[:, ring * 128 : (ring + 1) * 128]
            rows = slice(core * HALF, (core + 1) * HALF)
            out_ref[peer, at + ROWS : at + ROWS + HALF, :] = c_ref[rows, ring * 128 : (ring + 1) * 128]
            head = (ring * CORES + core) * MINE
            rest = jnp.zeros((MINE, 128 - 2 * ROWS), F32)
            both = jnp.concatenate([steps[head : head + MINE], decays[head : head + MINE], rest], 1)
            out_ref[peer, at + ROWS + HALF :, :] = both.astype(BF16)
    copies[4].wait()
    for core in range(CORES):
        for ring in range(RING):
            for tile in range(TILES):
                column = ring * CORES * WIDE + core * WIDE + tile * 128
                out_ref[core * RING + ring, tile * ROWS : (tile + 1) * ROWS, :] = x_ref[:, column : column + 128]
    rows = slice(ROWS - 16, ROWS)
    for leader in range(LEADERS):
        for member in range(MEMBERS):
            core, ring = member_of(leader, member)
            column = (ring * CORES + core) * WIDE
            pieces = [x_ref[rows, column + tile * 128 : column + (tile + 1) * 128] for tile in range(TILES)]
            pieces += [ref[rows, ring * 128 : (ring + 1) * 128] for ref in (b_ref, c_ref)]
            pieces = [piece.astype(F32) for piece in pieces]
            whole = [piece[16 - BORDER + token :][:1] for token in range(BORDER) for piece in pieces + pieces[:2]]
            rims[leader][member] = jnp.concatenate(whole, 0).astype(BF16)


def raw(r_ref, span, tile):
    return r_ref[span * FROM : (span + 1) * FROM, tile * ROWS : (tile + 1) * ROWS, :].reshape(SPAN, 128)


def c_rows(r_ref):
    at = (TILES + 1) * ROWS
    return r_ref[:, at : at + HALF, :]


def fill(r_ref, rims, pad_ref, tiles):
    rim = rims[0][0].astype(F32)
    for ref in rims[1:]:
        rim = rim + ref[...].astype(F32)
    for tile in tiles:
        tokens = [rim[token * 8 + tile : token * 8 + tile + 1] for token in range(BORDER)]
        edge = jnp.concatenate([jnp.zeros((8 - BORDER, 128), F32)] + tokens, 0)
        pad_ref[tile, 0:8, :] = edge
        if tile > TILES:
            continue
        for span in range(SPANS):
            pad_ref[tile, 8 + span * SPAN : 8 + (span + 1) * SPAN, :] = raw(r_ref, span, tile).astype(F32)


def conv_silu(taps_ref, pad_ref, span, tile):
    lanes = slice(tile * 128, (tile + 1) * 128)
    at = 8 - BORDER + span * SPAN
    total = pad_ref[tile, at : at + SPAN, :] * taps_ref[0:1, lanes]
    for tap in range(1, BORDER + 1):
        total = total + pad_ref[tile, at + tap : at + tap + SPAN, :] * taps_ref[tap : tap + 1, lanes]
    return silu(total).astype(BF16)


def rows_of(r_ref):
    at = (TILES + 1) * ROWS + HALF
    steps, decays = [], []
    for span in range(SPANS):
        parts = [r_ref[span * FROM + m, at : at + MINE, :].astype(F32) for m in range(FROM)]
        steps.append(jnp.concatenate([part[:, :ROWS] for part in parts], 1))
        decays.append(jnp.concatenate([part[:, ROWS : 2 * ROWS] for part in parts], 1))
    decays = jnp.concatenate(decays, 0)
    row = lax.broadcasted_iota(jnp.int32, (SPAN, SPAN), 0)
    column = lax.broadcasted_iota(jnp.int32, (SPAN, SPAN), 1)
    upper = (row <= column).astype(F32).astype(BF16)
    running = jnp.dot(decays.astype(BF16), upper, preferred_element_type=F32)
    return jnp.concatenate(steps, 0), running


def terms(x, count):
    parts = []
    for _ in range(count):
        parts.append(x.astype(BF16))
        x = x - parts[-1].astype(F32)
    return parts


def own_lanes(count):
    row = lax.broadcasted_iota(jnp.int32, (count * MINE, WIDE), 0)
    column = lax.broadcasted_iota(jnp.int32, (count * MINE, WIDE), 1)
    return (lax.rem(row, MINE) == lax.div(column, HEAD_DIM)).astype(F32).astype(BF16)


def widen(per_head, lanes, count):
    stack = jnp.concatenate([part.astype(F32) for part in terms(per_head, count)], 0).astype(BF16)
    return lax.dot_general(stack, lanes, (((0,), (0,)), ((), ())), preferred_element_type=F32)


def span_state(taps_ref, pad_ref, span, tail):
    b_conv = conv_silu(taps_ref, pad_ref, span, TILES)
    parts = [conv_silu(taps_ref, pad_ref, span, tile) for tile in range(TILES)]
    x_conv = jnp.concatenate(parts, 1)
    weighted = (x_conv.astype(F32) * tail).astype(BF16)
    b_turned = jnp.transpose(b_conv.astype(F32)).astype(BF16)
    return x_conv, b_conv, jnp.dot(b_turned, weighted, preferred_element_type=F32)


def of_span(x, span):
    return x[span * MINE : (span + 1) * MINE]


def state_kernel(r_ref, taps_ref, *rest):
    rims, (message_ref, half_ref, pad_ref) = rest[:MEMBERS], rest[MEMBERS:]
    half_ref[...] = c_rows(r_ref)
    fill(r_ref, rims, pad_ref, range(TILES + 1))
    steps, running = rows_of(r_ref)
    lanes = own_lanes(2)
    after = jnp.zeros((MINE, 1), F32)
    tails = []
    for span in reversed(range(SPANS)):
        here = of_span(running, span)
        tails.insert(0, jnp.exp(here[:, SPAN - 1 :] - here + after) * of_span(steps, span))
        after = after + here[:, SPAN - 1 :]
    scale = widen(jnp.exp(after + jnp.zeros((MINE, SPAN), F32)), lanes, 2)[:1]
    weighted, turned = [], []
    for span in range(SPANS):
        tail = widen(tails[span], lanes, 2)
        b_conv = conv_silu(taps_ref, pad_ref, span, TILES)
        x_conv = jnp.concatenate([conv_silu(taps_ref, pad_ref, span, tile) for tile in range(TILES)], 1)
        weighted.append((x_conv.astype(F32) * tail).astype(BF16))
        turned.append(jnp.transpose(b_conv.astype(F32)).astype(BF16))
    state = jnp.dot(jnp.concatenate(turned, 1), jnp.concatenate(weighted, 0), preferred_element_type=F32)
    coarse = scale.astype(BF16).astype(F32)
    tail = jnp.concatenate([coarse, scale - coarse, jnp.zeros((6, WIDE), F32)], 0)
    for tile in range(TILES):
        here = slice(tile * 128, (tile + 1) * 128)
        for cut in range(STATE // CUT):
            whole = jnp.concatenate([state[cut * CUT : (cut + 1) * CUT, here], tail[:, here]], 0)
            message_ref[tile * (STATE // CUT) + cut] = whole.astype(BF16)


def local_kernel(core_ref, r_ref, other_ref, taps_ref, *rest):
    rims, (part_ref, c_ref, scale_ref, pad_ref) = rest[:MEMBERS], rest[MEMBERS:]
    fill(r_ref, rims, pad_ref, range(TILES + 2))
    first = core_ref[0] == 0
    own, other = c_rows(r_ref).astype(F32), other_ref[...].astype(F32)
    whole = jnp.concatenate([jnp.where(first, own, other), jnp.where(first, other, own)], 1)
    pad_ref[TILES + 1, 8:, :] = whole.reshape(TOKENS, 128)
    row = lax.broadcasted_iota(jnp.int32, (SPAN, SPAN), 0)
    column = lax.broadcasted_iota(jnp.int32, (SPAN, SPAN), 1)
    causal = row >= column
    low = lax.broadcasted_iota(jnp.int32, (SPAN, 128), 1) < HEAD_DIM
    steps, running = rows_of(r_ref)
    lanes_two, lanes_three = own_lanes(2), own_lanes(3)
    tails = jnp.exp(running[:, SPAN - 1 :] - running) * steps
    turned = jnp.transpose(jnp.concatenate([running, jnp.zeros((SPAN - SPANS * MINE, SPAN), F32)], 0))
    before = jnp.zeros((MINE, 1), F32)
    state = None
    for span in range(SPANS):
        c_conv = conv_silu(taps_ref, pad_ref, span, TILES + 1)
        c_ref[span] = c_conv
        x_conv, b_conv, fresh = span_state(taps_ref, pad_ref, span, widen(of_span(tails, span), lanes_two, 2))
        scores = lax.dot_general(c_conv, b_conv, (((1,), (1,)), ((), ())), preferred_element_type=F32)
        here = of_span(running, span)
        grown = widen(jnp.exp(here), lanes_two, 2)
        scale_ref[span] = grown if span == 0 else widen(jnp.exp(here + before), lanes_two, 2)
        outs = []
        for tile in range(TILES):
            lanes = slice(tile * 128, (tile + 1) * 128)
            pair = []
            for head in (2 * tile, 2 * tile + 1):
                at = span * MINE + head
                gap = turned[:, at : at + 1] - running[at : at + 1]
                decay = jnp.exp(jnp.where(causal, gap, -1e30)) * steps[at : at + 1]
                pair.append((decay * scores).astype(BF16))
            both = jnp.dot(jnp.concatenate(pair, 0), x_conv[:, lanes], preferred_element_type=F32)
            outs.append(jnp.where(low, both[:SPAN], both[SPAN:]))
        out = jnp.concatenate(outs, 1) + x_conv.astype(F32) * taps_ref[4:5, :WIDE]
        if span:
            out = out + jnp.dot(c_conv, state.astype(BF16), preferred_element_type=F32) * grown
        part_ref[span] = out
        before = before + here[:, SPAN - 1 :]
        if span == 0:
            state = fresh
        elif span < SPANS - 1:
            state = state * grown[SPAN - 1 :] + fresh


def chain_kernel(all_ref, out_ref):
    state = jnp.zeros((CUT, 128), F32)
    for run in range(RUNS):
        out_ref[run] = state.astype(BF16)
        if run < RUNS - 1:
            here = all_ref[run].astype(F32)
            state = state * (here[CUT : CUT + 1] + here[CUT + 1 : CUT + 2]) + here[:CUT]


def finish_kernel(part_ref, c_ref, scale_ref, state_ref, out_ref):
    state = jnp.concatenate([state_ref[tile] for tile in range(TILES)], 1)
    for span in range(SPANS):
        inter = jnp.dot(c_ref[span], state, preferred_element_type=F32)
        out_ref[span * SPAN : (span + 1) * SPAN, :] = (part_ref[span] + inter * scale_ref[span]).astype(BF16)


def gate_kernel(z_ref, gain_ref, gate_ref, row_ref):
    gate_ref[...] = silu(z_ref[...].astype(F32))
    row_ref[...] = gain_ref[...].astype(F32)


def norm_kernel(values_ref, gate_ref, gain_ref, out_hbm, out_ref, sent):
    copies = []
    for group in range(GROUPS):
        whole = slice(group * CORES * WIDE, (group + 1) * CORES * WIDE)
        here = jnp.concatenate([values_ref[core * RING + group] for core in range(CORES)], 1)
        here = here.astype(F32) * gate_ref[:, whole]
        square = jnp.sum(here * here, axis=1, keepdims=True)
        scale = lax.rsqrt(square * (1.0 / (CORES * WIDE)) + 1e-05)
        out_ref[:, whole] = (here * scale * gain_ref[:, whole]).astype(BF16)
        copies.append(pltpu.make_async_copy(out_ref.at[:, whole], out_hbm.at[:, whole], sent.at[group]))
        copies[-1].start()
    for copy in copies:
        copy.wait()


def shards(
    x_stream,
    z_stream,
    b_stream,
    c_stream,
    dt_stream,
    decay_stream,
    kernel_x,
    kernel_b,
    kernel_c,
    skip_gain,
    norm_gain,
):
    core = lax.axis_index("core")
    streams = (x_stream, b_stream, c_stream, dt_stream, decay_stream)
    packed, *rims = call(
        pack_kernel,
        (like((PEERS, PACK, 128), BF16),) + (like((MEMBERS, RIM, 128), BF16),) * LEADERS,
        0,
        2 * PEERS * PACK * 256,
        [pltpu.VMEM(stream.shape, BF16) for stream in streams] + [pltpu.SemaphoreType.DMA((5,))],
        vmem=60,
        in_specs=[pl.BlockSpec(memory_space=pltpu.HBM)] * 5,
    )(*streams)
    got = lax.all_to_all(packed, ("core", "head"), split_axis=0, concat_axis=0, tiled=True)
    everyone = ("seq", "core", "head")
    led = None
    place = [[core * RING + ring for core, ring in (member_of(i, j) for j in range(MEMBERS))] for i in range(LEADERS)]
    for leader, rim in enumerate(rims):
        pairs = [(i * PEERS + PEERS - 1, (i + 1) * PEERS + place[leader][0]) for i in range(RUNS - 1)]
        came = lax.ppermute(rim, everyone, pairs)
        led = came if led is None else led + came
    handed = [led]
    for member in range(1, MEMBERS):
        pairs = [(i * PEERS + devices[0], i * PEERS + devices[member]) for i in range(RUNS) for devices in place]
        handed.append(lax.ppermute(led[member], everyone, pairs))
    taps_x = lax.dynamic_slice_in_dim(kernel_x, core * WIDE, WIDE, 1)
    skip = jnp.repeat(lax.dynamic_slice_in_dim(skip_gain, core * MINE, MINE), HEAD_DIM)
    taps = jnp.concatenate([taps_x, kernel_b, kernel_c], 1).astype(F32)
    skip_row = jnp.pad(skip, (0, 2 * STATE))[None]
    taps = jnp.concatenate([taps, skip_row, jnp.zeros((3, WIDE + 2 * STATE), F32)], 0)
    pad = pltpu.VMEM((TILES + 2, TOKENS + 8, 128), F32)
    width = HEADS * HEAD_DIM
    taps, gain_held = lax.optimization_barrier((taps, norm_gain.reshape(1, width)))
    message, half = call(
        state_kernel,
        (like((RUNS, CUT + 8, 128), BF16), like((PEERS, HALF, 128), BF16)),
        10**9,
        2 * 10**6,
        [pad],
    )(got, taps, *handed)
    slices = lax.all_to_all(message, "seq", split_axis=0, concat_axis=0, tiled=True)
    other = lax.ppermute(half, "core", [(0, 1), (1, 0)])
    vmem = pl.BlockSpec(memory_space=pltpu.VMEM)
    part, c_conv, scale = call(
        local_kernel,
        (
            like((SPANS, SPAN, WIDE), F32),
            like((SPANS, SPAN, STATE), BF16),
            like((SPANS, SPAN, WIDE), F32),
        ),
        10**9,
        8 * 10**6,
        [pad],
        in_specs=[pl.BlockSpec(memory_space=pltpu.SMEM)] + [vmem] * (3 + MEMBERS),
    )(core.astype(jnp.int32).reshape(1), got, other, taps, *handed)
    z_held, slices = lax.optimization_barrier((z_stream, slices))
    gate, gain = call(
        gate_kernel, (like((ROWS, width), F32), like((1, width), F32)), 10**7, 2 * 10**6
    )(z_held, gain_held)
    part, gate, gain = lax.optimization_barrier((part, gate, gain))
    chained = call(chain_kernel, like((RUNS, CUT, 128), BF16), 10**7, 10**6)(slices)
    state = lax.all_to_all(chained, "seq", split_axis=0, concat_axis=0, tiled=True)
    hbm = pl.BlockSpec(memory_space=pltpu.HBM)
    values = call(
        finish_kernel,
        like((TOKENS, WIDE), BF16),
        10**8,
        3 * 10**6,
    )(part, c_conv, scale, state.reshape(TILES, STATE, 128))
    home = lax.all_to_all(
        values.reshape(PEERS, ROWS, WIDE), ("core", "head"), split_axis=0, concat_axis=0, tiled=True
    )
    return call(
        norm_kernel,
        like((ROWS, width), BF16),
        10**7,
        2 * 10**6,
        [pltpu.VMEM((ROWS, width), BF16), pltpu.SemaphoreType.DMA((GROUPS,))],
        out_specs=hbm,
    )(home, gate, gain)


def solution(mesh):
    finer = Mesh(mesh.devices.reshape(RUNS, CORES, RING), ("seq", "core", "head"))
    rows = P(("seq", "core", "head"), None)
    in_specs = (rows,) * 6 + (P(None, "head"),) * 3 + (P("head"), P())
    return jax.shard_map(shards, mesh=finer, in_specs=in_specs, out_specs=rows, check_vma=False)
```

```python
import functools

import jax
import jax.numpy as jnp
from jax import lax
from jax.experimental import pallas as pl
from jax.experimental.pallas import tpu as pltpu
from jax.sharding import Mesh
from jax.sharding import PartitionSpec as P

HEADS = 128
HEAD_DIM = 64
STATE = 128
GROUPS = 8
SPAN = 128
CORES = 2
RING = 8
PEERS = CORES * RING
ROWS = 32
TOKENS = PEERS * ROWS
SPANS = TOKENS // SPAN
FROM = SPAN // ROWS
MINE = HEADS // PEERS
WIDE = MINE * HEAD_DIM
TILES = WIDE // 128
LEADERS = 4
MEMBERS = PEERS // LEADERS
BORDER = 3
RIM = 8 * BORDER
RUNS = 32
HALF = ROWS // CORES
PACK = ROWS * (TILES + 1) + HALF + MINE
CUT = STATE * TILES // RUNS
F32 = jnp.float32
BF16 = jnp.bfloat16
MIB = 1024 * 1024


def call(body, outs, flops, moved, scratch=(), vmem=16, **specs):
    return pl.pallas_call(
        body,
        **specs,
        out_shape=outs,
        scratch_shapes=list(scratch),
        compiler_params=pltpu.CompilerParams(vmem_limit_bytes=vmem * MIB),
        cost_estimate=pl.CostEstimate(flops=flops, bytes_accessed=moved, transcendentals=0),
    )


def like(shape, dtype):
    return jax.ShapeDtypeStruct(shape, dtype)


def silu(x):
    half = 0.5 * x
    return half * jnp.tanh(half) + half


def member_of(leader, member):
    core, side = divmod(leader, 2)
    return core, member if side else RING - 1 - member


def pack_kernel(x_hbm, b_hbm, c_hbm, dt_hbm, decay_hbm, out_ref, *rest):
    rims, (x_ref, b_ref, c_ref, dt_ref, decay_ref, arrived) = rest[:LEADERS], rest[LEADERS:]
    pairs = ((x_hbm, x_ref), (dt_hbm, dt_ref), (decay_hbm, decay_ref), (b_hbm, b_ref), (c_hbm, c_ref))
    copies = [pltpu.make_async_copy(a, b, arrived.at[i]) for i, (a, b) in enumerate(pairs)]
    for copy in copies:
        copy.start()
    copies[1].wait()
    copies[2].wait()
    steps = jnp.transpose(dt_ref[...].astype(F32))
    decays = jnp.transpose(decay_ref[...].astype(F32))
    at = TILES * ROWS
    for copy in copies[3:5]:
        copy.wait()
    for core in range(CORES):
        for ring in range(RING):
            peer = core * RING + ring
            out_ref[peer, at : at + ROWS, :] = b_ref[:, ring * 128 : (ring + 1) * 128]
            rows = slice(core * HALF, (core + 1) * HALF)
            out_ref[peer, at + ROWS : at + ROWS + HALF, :] = c_ref[rows, ring * 128 : (ring + 1) * 128]
            head = (ring * CORES + core) * MINE
            rest = jnp.zeros((MINE, 128 - 2 * ROWS), F32)
            both = jnp.concatenate([steps[head : head + MINE], decays[head : head + MINE], rest], 1)
            out_ref[peer, at + ROWS + HALF :, :] = both.astype(BF16)
    copies[0].wait()
    for core in range(CORES):
        for ring in range(RING):
            for tile in range(TILES):
                column = ring * CORES * WIDE + core * WIDE + tile * 128
                out_ref[core * RING + ring, tile * ROWS : (tile + 1) * ROWS, :] = x_ref[:, column : column + 128]
    rows = slice(ROWS - 16, ROWS)
    for leader in range(LEADERS):
        for member in range(MEMBERS):
            core, ring = member_of(leader, member)
            column = (ring * CORES + core) * WIDE
            pieces = [x_ref[rows, column + tile * 128 : column + (tile + 1) * 128] for tile in range(TILES)]
            pieces += [ref[rows, ring * 128 : (ring + 1) * 128] for ref in (b_ref, c_ref)]
            pieces = [piece.astype(F32) for piece in pieces]
            whole = [piece[16 - BORDER + token :][:1] for token in range(BORDER) for piece in pieces + pieces[:2]]
            rims[leader][member] = jnp.concatenate(whole, 0).astype(BF16)


def raw(r_ref, span, tile):
    return r_ref[span * FROM : (span + 1) * FROM, tile * ROWS : (tile + 1) * ROWS, :].reshape(SPAN, 128)


def c_rows(r_ref):
    at = (TILES + 1) * ROWS
    return r_ref[:, at : at + HALF, :]


def fill(r_ref, rims, pad_ref, tiles):
    rim = rims[0][0].astype(F32)
    for ref in rims[1:]:
        rim = rim + ref[...].astype(F32)
    for tile in tiles:
        tokens = [rim[token * 8 + tile : token * 8 + tile + 1] for token in range(BORDER)]
        edge = jnp.concatenate([jnp.zeros((8 - BORDER, 128), F32)] + tokens, 0)
        pad_ref[tile, 0:8, :] = edge
        if tile > TILES:
            continue
        for span in range(SPANS):
            pad_ref[tile, 8 + span * SPAN : 8 + (span + 1) * SPAN, :] = raw(r_ref, span, tile).astype(F32)


def conv_silu(taps_ref, pad_ref, span, tile):
    lanes = slice(tile * 128, (tile + 1) * 128)
    at = 8 - BORDER + span * SPAN
    total = pad_ref[tile, at : at + SPAN, :] * taps_ref[0:1, lanes]
    for tap in range(1, BORDER + 1):
        total = total + pad_ref[tile, at + tap : at + tap + SPAN, :] * taps_ref[tap : tap + 1, lanes]
    return silu(total).astype(BF16)


def rows_of(r_ref):
    at = (TILES + 1) * ROWS + HALF
    steps, decays = [], []
    for span in range(SPANS):
        parts = [r_ref[span * FROM + m, at : at + MINE, :].astype(F32) for m in range(FROM)]
        steps.append(jnp.concatenate([part[:, :ROWS] for part in parts], 1))
        decays.append(jnp.concatenate([part[:, ROWS : 2 * ROWS] for part in parts], 1))
    decays = jnp.concatenate(decays, 0)
    row = lax.broadcasted_iota(jnp.int32, (SPAN, SPAN), 0)
    column = lax.broadcasted_iota(jnp.int32, (SPAN, SPAN), 1)
    upper = (row <= column).astype(F32).astype(BF16)
    running = jnp.dot(decays.astype(BF16), upper, preferred_element_type=F32)
    return jnp.concatenate(steps, 0), running


def terms(x, count):
    parts = []
    for _ in range(count):
        parts.append(x.astype(BF16))
        x = x - parts[-1].astype(F32)
    return parts


def own_lanes(count):
    row = lax.broadcasted_iota(jnp.int32, (count * MINE, WIDE), 0)
    column = lax.broadcasted_iota(jnp.int32, (count * MINE, WIDE), 1)
    return (lax.rem(row, MINE) == lax.div(column, HEAD_DIM)).astype(F32).astype(BF16)


def widen(per_head, lanes, count):
    stack = jnp.concatenate([part.astype(F32) for part in terms(per_head, count)], 0).astype(BF16)
    return lax.dot_general(stack, lanes, (((0,), (0,)), ((), ())), preferred_element_type=F32)


def span_state(taps_ref, pad_ref, span, tail):
    b_conv = conv_silu(taps_ref, pad_ref, span, TILES)
    parts = [conv_silu(taps_ref, pad_ref, span, tile) for tile in range(TILES)]
    x_conv = jnp.concatenate(parts, 1)
    weighted = (x_conv.astype(F32) * tail).astype(BF16)
    b_turned = jnp.transpose(b_conv.astype(F32)).astype(BF16)
    return x_conv, b_conv, jnp.dot(b_turned, weighted, preferred_element_type=F32)


def of_span(x, span):
    return x[span * MINE : (span + 1) * MINE]


def state_kernel(r_ref, taps_ref, *rest):
    rims, (message_ref, half_ref, pad_ref) = rest[:MEMBERS], rest[MEMBERS:]
    half_ref[...] = c_rows(r_ref)
    fill(r_ref, rims, pad_ref, range(TILES + 1))
    steps, running = rows_of(r_ref)
    lanes = own_lanes(2)
    after = jnp.zeros((MINE, 1), F32)
    tails = []
    for span in reversed(range(SPANS)):
        here = of_span(running, span)
        tails.insert(0, jnp.exp(here[:, SPAN - 1 :] - here + after) * of_span(steps, span))
        after = after + here[:, SPAN - 1 :]
    scale = widen(jnp.exp(after + jnp.zeros((MINE, SPAN), F32)), lanes, 2)[:1]
    weighted, turned = [], []
    for span in range(SPANS):
        tail = widen(tails[span], lanes, 2)
        b_conv = conv_silu(taps_ref, pad_ref, span, TILES)
        x_conv = jnp.concatenate([conv_silu(taps_ref, pad_ref, span, tile) for tile in range(TILES)], 1)
        weighted.append((x_conv.astype(F32) * tail).astype(BF16))
        turned.append(b_conv)
    state = lax.dot_general(
        jnp.concatenate(turned, 0),
        jnp.concatenate(weighted, 0),
        (((0,), (0,)), ((), ())),
        preferred_element_type=F32,
    )
    coarse = scale.astype(BF16).astype(F32)
    tail = jnp.concatenate([coarse, scale - coarse, jnp.zeros((6, WIDE), F32)], 0)
    for tile in range(TILES):
        here = slice(tile * 128, (tile + 1) * 128)
        for cut in range(STATE // CUT):
            whole = jnp.concatenate([state[cut * CUT : (cut + 1) * CUT, here], tail[:, here]], 0)
            message_ref[tile * (STATE // CUT) + cut] = whole.astype(BF16)


def local_kernel(core_ref, r_ref, other_ref, taps_ref, *rest):
    rims, (part_ref, c_ref, scale_ref, pad_ref) = rest[:MEMBERS], rest[MEMBERS:]
    fill(r_ref, rims, pad_ref, range(TILES + 2))
    first = core_ref[0] == 0
    own, other = c_rows(r_ref).astype(F32), other_ref[...].astype(F32)
    whole = jnp.concatenate([jnp.where(first, own, other), jnp.where(first, other, own)], 1)
    pad_ref[TILES + 1, 8:, :] = whole.reshape(TOKENS, 128)
    row = lax.broadcasted_iota(jnp.int32, (SPAN, SPAN), 0)
    column = lax.broadcasted_iota(jnp.int32, (SPAN, SPAN), 1)
    causal = row >= column
    low = lax.broadcasted_iota(jnp.int32, (SPAN, 128), 1) < HEAD_DIM
    steps, running = rows_of(r_ref)
    lanes_two, lanes_three = own_lanes(2), own_lanes(3)
    tails = jnp.exp(running[:, SPAN - 1 :] - running) * steps
    turned = jnp.transpose(jnp.concatenate([running, jnp.zeros((SPAN - SPANS * MINE, SPAN), F32)], 0))
    before = jnp.zeros((MINE, 1), F32)
    state = None
    for span in range(SPANS):
        c_conv = conv_silu(taps_ref, pad_ref, span, TILES + 1)
        c_ref[span] = c_conv
        x_conv, b_conv, fresh = span_state(taps_ref, pad_ref, span, widen(of_span(tails, span), lanes_two, 2))
        scores = lax.dot_general(c_conv, b_conv, (((1,), (1,)), ((), ())), preferred_element_type=F32)
        here = of_span(running, span)
        grown = widen(jnp.exp(here), lanes_two, 2)
        scale_ref[span] = grown if span == 0 else widen(jnp.exp(here + before), lanes_two, 2)
        outs = []
        for tile in range(TILES):
            lanes = slice(tile * 128, (tile + 1) * 128)
            pair = []
            for head in (2 * tile, 2 * tile + 1):
                at = span * MINE + head
                gap = turned[:, at : at + 1] - running[at : at + 1]
                decay = jnp.exp(jnp.where(causal, gap, -1e30)) * steps[at : at + 1]
                pair.append((decay * scores).astype(BF16))
            both = jnp.dot(jnp.concatenate(pair, 0), x_conv[:, lanes], preferred_element_type=F32)
            outs.append(jnp.where(low, both[:SPAN], both[SPAN:]))
        out = jnp.concatenate(outs, 1) + x_conv.astype(F32) * taps_ref[4:5, :WIDE]
        if span:
            out = out + jnp.dot(c_conv, state.astype(BF16), preferred_element_type=F32) * grown
        part_ref[span] = out
        before = before + here[:, SPAN - 1 :]
        if span == 0:
            state = fresh
        elif span < SPANS - 1:
            state = state * grown[SPAN - 1 :] + fresh


def chain_kernel(all_ref, out_ref):
    state = jnp.zeros((CUT, 128), F32)
    for run in range(RUNS):
        out_ref[run] = state.astype(BF16)
        if run < RUNS - 1:
            here = all_ref[run].astype(F32)
            state = state * (here[CUT : CUT + 1] + here[CUT + 1 : CUT + 2]) + here[:CUT]


def finish_kernel(part_ref, c_ref, scale_ref, state_ref, out_ref):
    state = jnp.concatenate([state_ref[tile] for tile in range(TILES)], 1)
    for span in range(SPANS):
        inter = jnp.dot(c_ref[span], state, preferred_element_type=F32)
        out_ref[span * SPAN : (span + 1) * SPAN, :] = (part_ref[span] + inter * scale_ref[span]).astype(BF16)


def gate_kernel(z_ref, gain_ref, gate_ref, row_ref):
    gate_ref[...] = silu(z_ref[...].astype(F32))
    row_ref[...] = gain_ref[...].astype(F32)


def norm_kernel(values_ref, gate_ref, gain_ref, out_hbm, out_ref, sent):
    copies = []
    for group in range(GROUPS):
        whole = slice(group * CORES * WIDE, (group + 1) * CORES * WIDE)
        here = jnp.concatenate([values_ref[core * RING + group] for core in range(CORES)], 1)
        here = here.astype(F32) * gate_ref[:, whole]
        square = jnp.sum(here * here, axis=1, keepdims=True)
        scale = lax.rsqrt(square * (1.0 / (CORES * WIDE)) + 1e-05)
        out_ref[:, whole] = (here * scale * gain_ref[:, whole]).astype(BF16)
        copies.append(pltpu.make_async_copy(out_ref.at[:, whole], out_hbm.at[:, whole], sent.at[group]))
        copies[-1].start()
    for copy in copies:
        copy.wait()


def shards(
    x_stream,
    z_stream,
    b_stream,
    c_stream,
    dt_stream,
    decay_stream,
    kernel_x,
    kernel_b,
    kernel_c,
    skip_gain,
    norm_gain,
):
    core = lax.axis_index("core")
    streams = (x_stream, b_stream, c_stream, dt_stream, decay_stream)
    packed, *rims = call(
        pack_kernel,
        (like((PEERS, PACK, 128), BF16),) + (like((MEMBERS, RIM, 128), BF16),) * LEADERS,
        0,
        2 * PEERS * PACK * 256,
        [pltpu.VMEM(stream.shape, BF16) for stream in streams] + [pltpu.SemaphoreType.DMA((5,))],
        vmem=60,
        in_specs=[pl.BlockSpec(memory_space=pltpu.HBM)] * 5,
    )(*streams)
    got = lax.all_to_all(packed, ("core", "head"), split_axis=0, concat_axis=0, tiled=True)
    everyone = ("seq", "core", "head")
    led = None
    place = [[core * RING + ring for core, ring in (member_of(i, j) for j in range(MEMBERS))] for i in range(LEADERS)]
    for leader, rim in enumerate(rims):
        pairs = [(i * PEERS + PEERS - 1, (i + 1) * PEERS + place[leader][0]) for i in range(RUNS - 1)]
        came = lax.ppermute(rim, everyone, pairs)
        led = came if led is None else led + came
    handed = [led]
    for member in range(1, MEMBERS):
        pairs = [(i * PEERS + devices[0], i * PEERS + devices[member]) for i in range(RUNS) for devices in place]
        handed.append(lax.ppermute(led[member], everyone, pairs))
    taps_x = lax.dynamic_slice_in_dim(kernel_x, core * WIDE, WIDE, 1)
    skip = jnp.repeat(lax.dynamic_slice_in_dim(skip_gain, core * MINE, MINE), HEAD_DIM)
    taps = jnp.concatenate([taps_x, kernel_b, kernel_c], 1).astype(F32)
    skip_row = jnp.pad(skip, (0, 2 * STATE))[None]
    taps = jnp.concatenate([taps, skip_row, jnp.zeros((3, WIDE + 2 * STATE), F32)], 0)
    pad = pltpu.VMEM((TILES + 2, TOKENS + 8, 128), F32)
    width = HEADS * HEAD_DIM
    taps, gain_held = lax.optimization_barrier((taps, norm_gain.reshape(1, width)))
    message, half = call(
        state_kernel,
        (like((RUNS, CUT + 8, 128), BF16), like((PEERS, HALF, 128), BF16)),
        10**9,
        2 * 10**6,
        [pad],
    )(got, taps, *handed)
    slices = lax.all_to_all(message, "seq", split_axis=0, concat_axis=0, tiled=True)
    other = lax.ppermute(half, "core", [(0, 1), (1, 0)])
    vmem = pl.BlockSpec(memory_space=pltpu.VMEM)
    part, c_conv, scale = call(
        local_kernel,
        (
            like((SPANS, SPAN, WIDE), F32),
            like((SPANS, SPAN, STATE), BF16),
            like((SPANS, SPAN, WIDE), F32),
        ),
        10**9,
        8 * 10**6,
        [pad],
        in_specs=[pl.BlockSpec(memory_space=pltpu.SMEM)] + [vmem] * (3 + MEMBERS),
    )(core.astype(jnp.int32).reshape(1), got, other, taps, *handed)
    z_held, slices = lax.optimization_barrier((z_stream, slices))
    gate, gain = call(
        gate_kernel, (like((ROWS, width), F32), like((1, width), F32)), 10**7, 2 * 10**6
    )(z_held, gain_held)
    part, gate, gain = lax.optimization_barrier((part, gate, gain))
    chained = call(chain_kernel, like((RUNS, CUT, 128), BF16), 10**7, 10**6)(slices)
    state = lax.all_to_all(chained, "seq", split_axis=0, concat_axis=0, tiled=True)
    hbm = pl.BlockSpec(memory_space=pltpu.HBM)
    values = call(
        finish_kernel,
        like((TOKENS, WIDE), BF16),
        10**8,
        3 * 10**6,
    )(part, c_conv, scale, state.reshape(TILES, STATE, 128))
    home = lax.all_to_all(
        values.reshape(PEERS, ROWS, WIDE), ("core", "head"), split_axis=0, concat_axis=0, tiled=True
    )
    return call(
        norm_kernel,
        like((ROWS, width), BF16),
        10**7,
        2 * 10**6,
        [pltpu.VMEM((ROWS, width), BF16), pltpu.SemaphoreType.DMA((GROUPS,))],
        out_specs=hbm,
    )(home, gate, gain)


def solution(mesh):
    finer = Mesh(mesh.devices.reshape(RUNS, CORES, RING), ("seq", "core", "head"))
    rows = P(("seq", "core", "head"), None)
    in_specs = (rows,) * 6 + (P(None, "head"),) * 3 + (P("head"), P())
    return jax.shard_map(shards, mesh=finer, in_specs=in_specs, out_specs=rows, check_vma=False)
```

```python
import functools

import jax
import jax.numpy as jnp
from jax import lax
from jax.experimental import pallas as pl
from jax.experimental.pallas import tpu as pltpu
from jax.sharding import Mesh
from jax.sharding import PartitionSpec as P

HEADS = 128
HEAD_DIM = 64
STATE = 128
GROUPS = 8
SPAN = 128
CORES = 2
RING = 8
PEERS = CORES * RING
ROWS = 32
TOKENS = PEERS * ROWS
SPANS = TOKENS // SPAN
FROM = SPAN // ROWS
MINE = HEADS // PEERS
WIDE = MINE * HEAD_DIM
TILES = WIDE // 128
LEADERS = 4
MEMBERS = PEERS // LEADERS
BORDER = 3
RIM = 8 * BORDER
RUNS = 32
HALF = ROWS // CORES
PACK = ROWS * (TILES + 1) + HALF + MINE
CUT = STATE * TILES // RUNS
F32 = jnp.float32
BF16 = jnp.bfloat16
MIB = 1024 * 1024


def call(body, outs, flops, moved, scratch=(), vmem=16, **specs):
    return pl.pallas_call(
        body,
        **specs,
        out_shape=outs,
        scratch_shapes=list(scratch),
        compiler_params=pltpu.CompilerParams(vmem_limit_bytes=vmem * MIB),
        cost_estimate=pl.CostEstimate(flops=flops, bytes_accessed=moved, transcendentals=0),
    )


def like(shape, dtype):
    return jax.ShapeDtypeStruct(shape, dtype)


def silu(x):
    half = 0.5 * x
    return half * jnp.tanh(half) + half


def member_of(leader, member):
    core, side = divmod(leader, 2)
    return core, member if side else RING - 1 - member


def pack_kernel(x_hbm, b_hbm, c_hbm, dt_hbm, decay_hbm, out_ref, *rest):
    rims, (x_ref, b_ref, c_ref, dt_ref, decay_ref, arrived) = rest[:LEADERS], rest[LEADERS:]
    pairs = ((x_hbm, x_ref), (dt_hbm, dt_ref), (decay_hbm, decay_ref), (b_hbm, b_ref), (c_hbm, c_ref))
    copies = [pltpu.make_async_copy(a, b, arrived.at[i]) for i, (a, b) in enumerate(pairs)]
    for copy in copies:
        copy.start()
    copies[1].wait()
    copies[2].wait()
    steps = jnp.transpose(dt_ref[...].astype(F32))
    decays = jnp.transpose(decay_ref[...].astype(F32))
    at = TILES * ROWS
    for copy in copies[3:5]:
        copy.wait()
    for core in range(CORES):
        for ring in range(RING):
            peer = core * RING + ring
            out_ref[peer, at : at + ROWS, :] = b_ref[:, ring * 128 : (ring + 1) * 128]
            rows = slice(core * HALF, (core + 1) * HALF)
            out_ref[peer, at + ROWS : at + ROWS + HALF, :] = c_ref[rows, ring * 128 : (ring + 1) * 128]
            head = (ring * CORES + core) * MINE
            rest = jnp.zeros((MINE, 128 - 2 * ROWS), F32)
            both = jnp.concatenate([steps[head : head + MINE], decays[head : head + MINE], rest], 1)
            out_ref[peer, at + ROWS + HALF :, :] = both.astype(BF16)
    copies[0].wait()
    for core in range(CORES):
        for ring in range(RING):
            for tile in range(TILES):
                column = ring * CORES * WIDE + core * WIDE + tile * 128
                out_ref[core * RING + ring, tile * ROWS : (tile + 1) * ROWS, :] = x_ref[:, column : column + 128]
    rows = slice(ROWS - 16, ROWS)
    for leader in range(LEADERS):
        for member in range(MEMBERS):
            core, ring = member_of(leader, member)
            column = (ring * CORES + core) * WIDE
            pieces = [x_ref[rows, column + tile * 128 : column + (tile + 1) * 128] for tile in range(TILES)]
            pieces += [ref[rows, ring * 128 : (ring + 1) * 128] for ref in (b_ref, c_ref)]
            pieces = [piece.astype(F32) for piece in pieces]
            whole = [piece[16 - BORDER + token :][:1] for token in range(BORDER) for piece in pieces + pieces[:2]]
            rims[leader][member] = jnp.concatenate(whole, 0).astype(BF16)


def raw(r_ref, span, tile):
    return r_ref[span * FROM : (span + 1) * FROM, tile * ROWS : (tile + 1) * ROWS, :].reshape(SPAN, 128)


def c_rows(r_ref):
    at = (TILES + 1) * ROWS
    return r_ref[:, at : at + HALF, :]


def fill(r_ref, rims, pad_ref, tiles):
    rim = rims[0][0].astype(F32)
    for ref in rims[1:]:
        rim = rim + ref[...].astype(F32)
    for tile in tiles:
        tokens = [rim[token * 8 + tile : token * 8 + tile + 1] for token in range(BORDER)]
        edge = jnp.concatenate([jnp.zeros((8 - BORDER, 128), F32)] + tokens, 0)
        pad_ref[tile, 0:8, :] = edge
        if tile > TILES:
            continue
        for span in range(SPANS):
            pad_ref[tile, 8 + span * SPAN : 8 + (span + 1) * SPAN, :] = raw(r_ref, span, tile).astype(F32)


def conv_silu(taps_ref, pad_ref, span, tile):
    lanes = slice(tile * 128, (tile + 1) * 128)
    at = 8 - BORDER + span * SPAN
    total = pad_ref[tile, at : at + SPAN, :] * taps_ref[0:1, lanes]
    for tap in range(1, BORDER + 1):
        total = total + pad_ref[tile, at + tap : at + tap + SPAN, :] * taps_ref[tap : tap + 1, lanes]
    return silu(total).astype(BF16)


def rows_of(r_ref):
    at = (TILES + 1) * ROWS + HALF
    steps, decays = [], []
    for span in range(SPANS):
        parts = [r_ref[span * FROM + m, at : at + MINE, :].astype(F32) for m in range(FROM)]
        steps.append(jnp.concatenate([part[:, :ROWS] for part in parts], 1))
        decays.append(jnp.concatenate([part[:, ROWS : 2 * ROWS] for part in parts], 1))
    decays = jnp.concatenate(decays, 0)
    row = lax.broadcasted_iota(jnp.int32, (SPAN, SPAN), 0)
    column = lax.broadcasted_iota(jnp.int32, (SPAN, SPAN), 1)
    upper = (row <= column).astype(F32).astype(BF16)
    running = jnp.dot(decays.astype(BF16), upper, preferred_element_type=F32)
    return jnp.concatenate(steps, 0), running


def terms(x, count):
    parts = []
    for _ in range(count):
        parts.append(x.astype(BF16))
        x = x - parts[-1].astype(F32)
    return parts


def own_lanes(count):
    row = lax.broadcasted_iota(jnp.int32, (count * MINE, WIDE), 0)
    column = lax.broadcasted_iota(jnp.int32, (count * MINE, WIDE), 1)
    return (lax.rem(row, MINE) == lax.div(column, HEAD_DIM)).astype(F32).astype(BF16)


def widen(per_head, lanes, count):
    stack = jnp.concatenate([part.astype(F32) for part in terms(per_head, count)], 0).astype(BF16)
    return lax.dot_general(stack, lanes, (((0,), (0,)), ((), ())), preferred_element_type=F32)


def span_state(taps_ref, pad_ref, span, tail):
    b_conv = conv_silu(taps_ref, pad_ref, span, TILES)
    parts = [conv_silu(taps_ref, pad_ref, span, tile) for tile in range(TILES)]
    x_conv = jnp.concatenate(parts, 1)
    weighted = (x_conv.astype(F32) * tail).astype(BF16)
    b_turned = jnp.transpose(b_conv.astype(F32)).astype(BF16)
    return x_conv, b_conv, jnp.dot(b_turned, weighted, preferred_element_type=F32)


def of_span(x, span):
    return x[span * MINE : (span + 1) * MINE]


def state_kernel(r_ref, taps_ref, *rest):
    rims, (message_ref, half_ref, pad_ref) = rest[:MEMBERS], rest[MEMBERS:]
    half_ref[...] = c_rows(r_ref)
    fill(r_ref, rims, pad_ref, range(TILES + 1))
    steps, running = rows_of(r_ref)
    lanes = own_lanes(2)
    after = jnp.zeros((MINE, 1), F32)
    tails = []
    for span in reversed(range(SPANS)):
        here = of_span(running, span)
        tails.insert(0, jnp.exp(here[:, SPAN - 1 :] - here + after) * of_span(steps, span))
        after = after + here[:, SPAN - 1 :]
    scale = widen(jnp.exp(after + jnp.zeros((MINE, SPAN), F32)), lanes, 2)[:1]
    weighted, turned = [], []
    for span in range(SPANS):
        tail = widen(tails[span], lanes, 2)
        b_conv = conv_silu(taps_ref, pad_ref, span, TILES)
        x_conv = jnp.concatenate([conv_silu(taps_ref, pad_ref, span, tile) for tile in range(TILES)], 1)
        weighted.append((x_conv.astype(F32) * tail).astype(BF16))
        turned.append(b_conv)
    state = lax.dot_general(
        jnp.concatenate(turned, 0),
        jnp.concatenate(weighted, 0),
        (((0,), (0,)), ((), ())),
        preferred_element_type=F32,
    )
    coarse = scale.astype(BF16).astype(F32)
    tail = jnp.concatenate([coarse, scale - coarse, jnp.zeros((6, WIDE), F32)], 0).astype(BF16)
    state = state.astype(BF16)
    for tile in range(TILES):
        here = slice(tile * 128, (tile + 1) * 128)
        for cut in range(STATE // CUT):
            message_ref[tile * (STATE // CUT) + cut, :CUT] = state[cut * CUT : (cut + 1) * CUT, here]
            message_ref[tile * (STATE // CUT) + cut, CUT:] = tail[:, here]


def local_kernel(core_ref, r_ref, other_ref, taps_ref, *rest):
    rims, (part_ref, c_ref, scale_ref, pad_ref) = rest[:MEMBERS], rest[MEMBERS:]
    fill(r_ref, rims, pad_ref, range(TILES + 2))
    first = core_ref[0] == 0
    own, other = c_rows(r_ref).astype(F32), other_ref[...].astype(F32)
    whole = jnp.concatenate([jnp.where(first, own, other), jnp.where(first, other, own)], 1)
    pad_ref[TILES + 1, 8:, :] = whole.reshape(TOKENS, 128)
    row = lax.broadcasted_iota(jnp.int32, (SPAN, SPAN), 0)
    column = lax.broadcasted_iota(jnp.int32, (SPAN, SPAN), 1)
    causal = row >= column
    low = lax.broadcasted_iota(jnp.int32, (SPAN, 128), 1) < HEAD_DIM
    steps, running = rows_of(r_ref)
    lanes_two, lanes_three = own_lanes(2), own_lanes(3)
    tails = jnp.exp(running[:, SPAN - 1 :] - running) * steps
    turned = jnp.transpose(jnp.concatenate([running, jnp.zeros((SPAN - SPANS * MINE, SPAN), F32)], 0))
    before = jnp.zeros((MINE, 1), F32)
    state = None
    for span in range(SPANS):
        c_conv = conv_silu(taps_ref, pad_ref, span, TILES + 1)
        c_ref[span] = c_conv
        x_conv, b_conv, fresh = span_state(taps_ref, pad_ref, span, widen(of_span(tails, span), lanes_two, 2))
        scores = lax.dot_general(c_conv, b_conv, (((1,), (1,)), ((), ())), preferred_element_type=F32)
        here = of_span(running, span)
        grown = widen(jnp.exp(here), lanes_two, 2)
        scale_ref[span] = grown if span == 0 else widen(jnp.exp(here + before), lanes_two, 2)
        outs = []
        for tile in range(TILES):
            lanes = slice(tile * 128, (tile + 1) * 128)
            pair = []
            for head in (2 * tile, 2 * tile + 1):
                at = span * MINE + head
                gap = turned[:, at : at + 1] - running[at : at + 1]
                decay = jnp.exp(jnp.where(causal, gap, -1e30)) * steps[at : at + 1]
                pair.append((decay * scores).astype(BF16))
            both = jnp.dot(jnp.concatenate(pair, 0), x_conv[:, lanes], preferred_element_type=F32)
            outs.append(jnp.where(low, both[:SPAN], both[SPAN:]))
        out = jnp.concatenate(outs, 1) + x_conv.astype(F32) * taps_ref[4:5, :WIDE]
        if span:
            out = out + jnp.dot(c_conv, state.astype(BF16), preferred_element_type=F32) * grown
        part_ref[span] = out
        before = before + here[:, SPAN - 1 :]
        if span == 0:
            state = fresh
        elif span < SPANS - 1:
            state = state * grown[SPAN - 1 :] + fresh


def chain_kernel(all_ref, out_ref):
    state = jnp.zeros((CUT, 128), F32)
    for run in range(RUNS):
        out_ref[run] = state.astype(BF16)
        if run < RUNS - 1:
            here = all_ref[run].astype(F32)
            state = state * (here[CUT : CUT + 1] + here[CUT + 1 : CUT + 2]) + here[:CUT]


def finish_kernel(part_ref, c_ref, scale_ref, state_ref, out_ref):
    state = jnp.concatenate([state_ref[tile] for tile in range(TILES)], 1)
    for span in range(SPANS):
        inter = jnp.dot(c_ref[span], state, preferred_element_type=F32)
        out_ref[span * SPAN : (span + 1) * SPAN, :] = (part_ref[span] + inter * scale_ref[span]).astype(BF16)


def gate_kernel(z_ref, gain_ref, gate_ref, row_ref):
    gate_ref[...] = silu(z_ref[...].astype(F32))
    row_ref[...] = gain_ref[...].astype(F32)


def norm_kernel(values_ref, gate_ref, gain_ref, out_hbm, out_ref, sent):
    copies = []
    for group in range(GROUPS):
        whole = slice(group * CORES * WIDE, (group + 1) * CORES * WIDE)
        here = jnp.concatenate([values_ref[core * RING + group] for core in range(CORES)], 1)
        here = here.astype(F32) * gate_ref[:, whole]
        square = jnp.sum(here * here, axis=1, keepdims=True)
        scale = lax.rsqrt(square * (1.0 / (CORES * WIDE)) + 1e-05)
        out_ref[:, whole] = (here * scale * gain_ref[:, whole]).astype(BF16)
        copies.append(pltpu.make_async_copy(out_ref.at[:, whole], out_hbm.at[:, whole], sent.at[group]))
        copies[-1].start()
    for copy in copies:
        copy.wait()


def shards(
    x_stream,
    z_stream,
    b_stream,
    c_stream,
    dt_stream,
    decay_stream,
    kernel_x,
    kernel_b,
    kernel_c,
    skip_gain,
    norm_gain,
):
    core = lax.axis_index("core")
    streams = (x_stream, b_stream, c_stream, dt_stream, decay_stream)
    packed, *rims = call(
        pack_kernel,
        (like((PEERS, PACK, 128), BF16),) + (like((MEMBERS, RIM, 128), BF16),) * LEADERS,
        0,
        2 * PEERS * PACK * 256,
        [pltpu.VMEM(stream.shape, BF16) for stream in streams] + [pltpu.SemaphoreType.DMA((5,))],
        vmem=60,
        in_specs=[pl.BlockSpec(memory_space=pltpu.HBM)] * 5,
    )(*streams)
    got = lax.all_to_all(packed, ("core", "head"), split_axis=0, concat_axis=0, tiled=True)
    everyone = ("seq", "core", "head")
    led = None
    place = [[core * RING + ring for core, ring in (member_of(i, j) for j in range(MEMBERS))] for i in range(LEADERS)]
    for leader, rim in enumerate(rims):
        pairs = [(i * PEERS + PEERS - 1, (i + 1) * PEERS + place[leader][0]) for i in range(RUNS - 1)]
        came = lax.ppermute(rim, everyone, pairs)
        led = came if led is None else led + came
    handed = [led]
    for member in range(1, MEMBERS):
        pairs = [(i * PEERS + devices[0], i * PEERS + devices[member]) for i in range(RUNS) for devices in place]
        handed.append(lax.ppermute(led[member], everyone, pairs))
    taps_x = lax.dynamic_slice_in_dim(kernel_x, core * WIDE, WIDE, 1)
    skip = jnp.repeat(lax.dynamic_slice_in_dim(skip_gain, core * MINE, MINE), HEAD_DIM)
    taps = jnp.concatenate([taps_x, kernel_b, kernel_c], 1).astype(F32)
    skip_row = jnp.pad(skip, (0, 2 * STATE))[None]
    taps = jnp.concatenate([taps, skip_row, jnp.zeros((3, WIDE + 2 * STATE), F32)], 0)
    pad = pltpu.VMEM((TILES + 2, TOKENS + 8, 128), F32)
    width = HEADS * HEAD_DIM
    taps, gain_held = lax.optimization_barrier((taps, norm_gain.reshape(1, width)))
    message, half = call(
        state_kernel,
        (like((RUNS, CUT + 8, 128), BF16), like((PEERS, HALF, 128), BF16)),
        10**9,
        2 * 10**6,
        [pad],
    )(got, taps, *handed)
    slices = lax.all_to_all(message, "seq", split_axis=0, concat_axis=0, tiled=True)
    other = lax.ppermute(half, "core", [(0, 1), (1, 0)])
    vmem = pl.BlockSpec(memory_space=pltpu.VMEM)
    part, c_conv, scale = call(
        local_kernel,
        (
            like((SPANS, SPAN, WIDE), F32),
            like((SPANS, SPAN, STATE), BF16),
            like((SPANS, SPAN, WIDE), F32),
        ),
        10**9,
        8 * 10**6,
        [pad],
        in_specs=[pl.BlockSpec(memory_space=pltpu.SMEM)] + [vmem] * (3 + MEMBERS),
    )(core.astype(jnp.int32).reshape(1), got, other, taps, *handed)
    z_held, slices = lax.optimization_barrier((z_stream, slices))
    gate, gain = call(
        gate_kernel, (like((ROWS, width), F32), like((1, width), F32)), 10**7, 2 * 10**6
    )(z_held, gain_held)
    part, gate, gain = lax.optimization_barrier((part, gate, gain))
    chained = call(chain_kernel, like((RUNS, CUT, 128), BF16), 10**7, 10**6)(slices)
    state = lax.all_to_all(chained, "seq", split_axis=0, concat_axis=0, tiled=True)
    hbm = pl.BlockSpec(memory_space=pltpu.HBM)
    values = call(
        finish_kernel,
        like((TOKENS, WIDE), BF16),
        10**8,
        3 * 10**6,
    )(part, c_conv, scale, state.reshape(TILES, STATE, 128))
    home = lax.all_to_all(
        values.reshape(PEERS, ROWS, WIDE), ("core", "head"), split_axis=0, concat_axis=0, tiled=True
    )
    return call(
        norm_kernel,
        like((ROWS, width), BF16),
        10**7,
        2 * 10**6,
        [pltpu.VMEM((ROWS, width), BF16), pltpu.SemaphoreType.DMA((GROUPS,))],
        out_specs=hbm,
    )(home, gate, gain)


def solution(mesh):
    finer = Mesh(mesh.devices.reshape(RUNS, CORES, RING), ("seq", "core", "head"))
    rows = P(("seq", "core", "head"), None)
    in_specs = (rows,) * 6 + (P(None, "head"),) * 3 + (P("head"), P())
    return jax.shard_map(shards, mesh=finer, in_specs=in_specs, out_specs=rows, check_vma=False)
```
